512 devices in a mesh: section: 32 (over z_lo, y, core), tensor: 16 (over z_hi, x).
Axes of the slice: x: 4, y: 4, z: 16 (z_hi: 4, z_lo: 4; z = z_hi * 4 + z_lo), core: 2. Of those that a mesh axis runs over, the one named last changes fastest.
Arguments:
- layer_input: bfloat16 [768, 8192], P(None, 'section'), may hold values from -6 to 6
- w_up: bfloat16 [8192, 16384], P('section', 'tensor'), may hold values from -0.09375 to 0.09375
- w_down: bfloat16 [8192, 16384], P('section', 'tensor'), may hold values from -0.046875 to 0.046875
- parked_codes: bfloat16 [1536, 16384], P('section', 'tensor'), may hold values from -127 to 127, as said below
- parked_scales: bfloat16 [1536], P('section'), may hold values from 0.0039978027 to 0.029907227
- parked_rows: int32 [1536], P('section'), may hold values from 0 to 767, as said below
- incoming: bfloat16 [768, 8192], P(None, 'section'), may hold values from -6 to 6
Outputs:
- grad_up: bfloat16 [8192, 16384], P('section', 'tensor')
- grad_down: bfloat16 [8192, 16384], P('section', 'tensor')
- passed: bfloat16 [768, 8192], P(None, 'section')
The draws below stay inside these ranges and needn't reach their ends.
Inputs may be any that keep to these rules, and one draw needn't show every extreme that they name: `parked_codes`: integer values. `parked_rows`: each aligned block of 768 entries (one section) is a permutation of 0 to 767.
All inputs are finite; a program needn't handle non-finite values.
Results may differ from the reference program's by a relative error of at most 0.005.
Values may be sent and summed in bfloat16 or wider, within the bound.
No kernel may reach another device: no remote copies, remote signals or barrier semaphores. Data moves between devices by JAX's collectives and lax.ppermute only.
A program may use at most 64 MiB of HBM per device.

```python
import math
import jax
import jax.numpy as jnp
from jax import lax

D = 4096
SECTIONS = 2
MICRO = 768
FF = 16384
ROWS = 1536


def draw_parked_codes(key, part):
    key = jax.random.fold_in(key, 11)
    return jax.random.randint(key, (ROWS, FF), -127, 128).astype(jnp.float32).astype(jnp.bfloat16)


def draw_parked_rows(key, part):
    key = jax.random.fold_in(key, 23)
    section_keys = jax.random.split(key, SECTIONS)
    orders = jax.vmap(lambda k: jax.random.permutation(k, MICRO))(section_keys)
    return orders.reshape(ROWS).astype(jnp.int32)


def steps_of(rng, extent, pieces, least, high):
    loudness = 1.0
    for position, parts in pieces:
        steps = jax.random.uniform(jax.random.fold_in(jax.random.fold_in(rng, 6), position), (parts,), jnp.float32, least / len(pieces), high / len(pieces))
        loudness = loudness * jnp.repeat(jnp.exp(steps), extent[position] // parts).reshape((-1,) + (1,) * (len(extent) - 1 - position))
    return loudness


def gaussian(stream_key, dims, deviation, limit, shards=(), kind=jnp.bfloat16):
    result = jax.random.normal(stream_key, dims, jnp.float32) * deviation
    if len(shards) > 0:
        result = steps_of(stream_key, dims, shards, -0.22, 0.18) * result
    return jnp.clip(result, min=-limit, max=limit).astype(kind)


def setup_inputs(seed: int = 0) -> dict:
    streams_of = jax.random.split(jax.random.key(seed), 8)
    layer_input = gaussian(streams_of[0], (MICRO, SECTIONS * D), 1.0, 6.0, ((1, 32),))
    w_up = gaussian(streams_of[1], (SECTIONS * D, FF), D ** -0.5, 0.09375, ((0, 32), (1, 16)))
    w_down = gaussian(streams_of[2], (SECTIONS * D, FF), FF ** -0.5, 0.046875, ((0, 32), (1, 16)))
    parked_codes = draw_parked_codes(jax.random.fold_in(streams_of[7], 71), 0)
    parked_scales = jnp.clip(jnp.exp(math.log(0.029907227) - 2.01235525 * jax.random.uniform(streams_of[4], (ROWS,), jnp.float32) ** steps_of(streams_of[4], (ROWS,), ((0, 32),), -0.2, 0.2)), 0.0039978027, 0.029907227).astype(jnp.bfloat16)
    parked_rows = draw_parked_rows(jax.random.fold_in(streams_of[7], 71), 0)
    incoming = gaussian(streams_of[6], (MICRO, SECTIONS * D), 1.0, 6.0, ((1, 32),))
    return dict(layer_input=layer_input, w_up=w_up, w_down=w_down, parked_codes=parked_codes, parked_scales=parked_scales, parked_rows=parked_rows, incoming=incoming)


def section_backward(operands):
    layer_x, up_weight, down_weight, codes, scales, rows, grad_out = operands
    values = codes.astype(jnp.float32) * scales.astype(jnp.float32)[:, None]
    hidden_in = jnp.zeros(values.shape, jnp.float32).at[rows].set(values)
    activated = jax.nn.gelu(hidden_in, approximate=False).astype(jnp.bfloat16)
    act_grad = jnp.dot(grad_out, down_weight, preferred_element_type=jnp.float32)
    density = jnp.exp(-0.5 * hidden_in * hidden_in) * 0.3989422804014327
    cumulative = 0.5 * (1.0 + lax.erf(hidden_in * 0.7071067811865476))
    hidden_grad = (act_grad * (cumulative + hidden_in * density)).astype(jnp.bfloat16)
    grad_down = jnp.dot(grad_out.T, activated, preferred_element_type=jnp.float32).astype(jnp.bfloat16)
    grad_up = jnp.dot(layer_x.T, hidden_grad, preferred_element_type=jnp.float32).astype(jnp.bfloat16)
    input_grad = jnp.dot(hidden_grad, up_weight.T, preferred_element_type=jnp.float32)
    section_grad = (grad_out.astype(jnp.float32) + input_grad).astype(jnp.bfloat16)
    return grad_up, grad_down, section_grad


def reference(layer_input, w_up, w_down, parked_codes, parked_scales, parked_rows, incoming):
    layer_x = layer_input.reshape(MICRO, SECTIONS, D).transpose(1, 0, 2)
    grad_out = incoming.reshape(MICRO, SECTIONS, D).transpose(1, 0, 2)
    up_all = w_up.reshape(SECTIONS, D, FF)
    down_all = w_down.reshape(SECTIONS, D, FF)
    codes = parked_codes.reshape(SECTIONS, MICRO, FF)[::-1]
    scales = parked_scales.reshape(SECTIONS, MICRO)[::-1]
    rows = parked_rows.reshape(SECTIONS, MICRO)[::-1].astype(jnp.int32)
    grad_up, grad_down, section_grad = lax.map(section_backward, (layer_x, up_all, down_all, codes, scales, rows, grad_out))
    shifted = jnp.concatenate([section_grad[1:], jnp.zeros((1, MICRO, D), jnp.bfloat16)], axis=0)
    passed = shifted.transpose(1, 0, 2).reshape(MICRO, SECTIONS * D)
    return grad_up.reshape(SECTIONS * D, FF), grad_down.reshape(SECTIONS * D, FF), passed
```

```python
import functools
import math

import jax
import jax.numpy as jnp
from jax import lax
from jax.experimental import pallas as pl
from jax.experimental.pallas import tpu as pltpu
from jax.sharding import Mesh, PartitionSpec as P

SHAPE = (2, 2, 4, 2, 4, 4)
NAMES = ("half", "zb", "y", "core", "zh", "x")
SECTION = ("half", "zb", "y", "core")
TENSOR = ("zh", "x")
CHIPS = ("zb", "y")
F32 = jnp.float32
BF16 = jnp.bfloat16
TOK = 768
HALF = 384
OWN = 48
PACK = 64
SMEM = pl.BlockSpec(memory_space=pltpu.SMEM)
VMEM = pl.BlockSpec(memory_space=pltpu.VMEM)
PARAMS = pltpu.CompilerParams(vmem_limit_bytes=48 * 1024 * 1024)


def call(kernel, shape, dtype, ins, scratch=(), flops=0, nbytes=0):
    return pl.pallas_call(
        kernel,
        out_shape=jax.ShapeDtypeStruct(shape, dtype),
        in_specs=[SMEM] + [VMEM] * (len(ins) - 1),
        out_specs=VMEM,
        scratch_shapes=list(scratch),
        compiler_params=PARAMS,
        cost_estimate=pl.CostEstimate(flops=flops, bytes_accessed=nbytes, transcendentals=0),
    )(*ins)


def swap(value, axis):
    return lax.ppermute(value, axis, [(0, 1), (1, 0)])


def dot(a, b, ca, cb):
    return lax.dot_general(a, b, (((ca,), (cb,)), ((), ())), preferred_element_type=F32)


def front(pos, g, g_far, v, v_far, pack, pack_far, out):
    core = pos[0]
    mine = g[pl.ds(pl.multiple_of(core * HALF, HALF), HALF), :]
    far = g_far[...]
    for j in range(4):
        cols = slice(256 * j, 256 * j + 256)
        part = dot(mine, v[:, cols], 1, 0) + dot(far, v_far[:, cols], 1, 0)
        part = part.astype(BF16)
        out[2 * j, :HALF, :] = part[:, :128]
        out[2 * j + 1, :HALF, :] = part[:, 128:]
    near_at = pl.multiple_of(HALF + PACK * core, PACK)
    far_at = pl.multiple_of(HALF + PACK * (1 - core), PACK)
    for i in range(8):
        cols = slice(128 * i, 128 * i + 128)
        out[i, pl.ds(near_at, PACK), :] = pack[:, cols]
        out[i, pl.ds(far_at, PACK), :] = pack_far[:, cols]


def rows_of(near, far):
    lane = lax.broadcasted_iota(jnp.int32, (1, 128), 1)
    low = lane < PACK

    def line(k):
        return jnp.where(low, near[k : k + 1, :].astype(F32), far[k : k + 1, :].astype(F32))

    token = (line(0) * 32.0 + line(1)).astype(jnp.int32)
    valid = (lane % PACK) < OWN
    return jnp.where(valid, token, -1), line(2)


def slope(pos, recv, out):
    core = pos[0]
    act = jnp.zeros((HALF, 128), F32)
    hidden = jnp.zeros((HALF, 128), F32)
    scale = jnp.zeros((HALF, 128), F32)
    token = lax.broadcasted_iota(jnp.int32, (HALF, 128), 0) + core * HALF
    for i in range(8):
        act = act + recv[i, :HALF, :].astype(F32)
        near = recv[i, HALF + OWN : HALF + PACK, :]
        far = recv[i, HALF + PACK + OWN : HALF + 2 * PACK, :]
        rows, scales = rows_of(near, far)
        hit = token == rows
        one = jnp.where(hit, 1.0, 0.0).astype(BF16)
        hidden = hidden + dot(one, recv[i, HALF:, :], 1, 0)
        scale = scale + jnp.where(hit, scales, 0.0)
    hidden = hidden * jnp.sum(scale, axis=1, keepdims=True)
    density = jnp.exp(-0.5 * hidden * hidden) * 0.3989422804014327
    cumulative = 0.5 * (1.0 + lax.erf(hidden * 0.7071067811865476))
    grad = (act * (cumulative + hidden * density)).astype(BF16)
    for i in range(8):
        out[i] = grad


def input_part(pos, hg, u, u_far, out):
    core = pos[0]
    rows = jnp.concatenate([hg[i] for i in range(8)], axis=1)
    near_at = pl.multiple_of(256 * core, 256)
    far_at = pl.multiple_of(256 * (1 - core), 256)
    out[:, pl.ds(near_at, 256)] = dot(rows, u[...], 1, 1).astype(BF16)
    out[:, pl.ds(far_at, 256)] = dot(rows, u_far[...], 1, 1).astype(BF16)


def add_x(pos, recv, g, g_far, out):
    core, x, first = pos[0], pos[1], pos[2] == 0
    total = recv[0].astype(F32)
    for i in range(1, 4):
        total = total + recv[i].astype(F32)
    near_at = pl.multiple_of(256 * core, 256)
    far_at = pl.multiple_of(256 * (1 - core), 256)
    mine = g[pl.ds(pl.multiple_of(core * HALF + x * 96, 96), 96), :].astype(F32)
    far = g_far[pl.ds(pl.multiple_of(x * 96, 96), 96), :].astype(F32)
    out[...] = total.astype(BF16)

    @pl.when(first)
    def _():
        both = jnp.where(core == 0, jnp.concatenate([mine, far], 1), jnp.concatenate([far, mine], 1))
        out[...] = (total + both).astype(BF16)


def add_z(pos, a, b, c, d, out):
    total = a[...].astype(F32) + b[...].astype(F32) + c[...].astype(F32) + d[...].astype(F32)
    total = total.astype(BF16)
    for i in range(4):
        out[i] = total[:, :256]
        out[4 + i] = total[:, 256:]


def down(pos, recv, g, act, out, held):
    token = lax.broadcasted_iota(jnp.int32, (TOK, 128), 0)
    for i in range(8):
        near = recv[i, HALF + OWN : HALF + PACK, :]
        far = recv[i, HALF + PACK + OWN : HALF + 2 * PACK, :]
        rows, _ = rows_of(near, far)
        one = jnp.where(token == rows, 1.0, 0.0).astype(BF16)
        moved = dot(one, g[...], 0, 0).astype(BF16)
        held[96 * i : 96 * i + OWN, :] = moved[:OWN]
        held[96 * i + OWN : 96 * i + 96, :] = moved[PACK : PACK + OWN]
    turned = held[...].T
    for j in range(4):
        cols = slice(256 * j, 256 * j + 256)
        out[:, cols] = dot(turned, act[:, cols], 1, 0).astype(BF16)


def up(pos, x, hg, hg_far, out):
    core = pos[0]
    mine = x[pl.ds(pl.multiple_of(core * HALF, HALF), HALF), :].T
    far = x[pl.ds(pl.multiple_of((1 - core) * HALF, HALF), HALF), :].T
    for j in range(4):
        near_hg = jnp.concatenate([hg[2 * j], hg[2 * j + 1]], axis=1)
        far_hg = jnp.concatenate([hg_far[2 * j], hg_far[2 * j + 1]], axis=1)
        part = dot(mine, near_hg, 1, 0) + dot(far, far_hg, 1, 0)
        out[:, 256 * j : 256 * j + 256] = part.astype(BF16)


def shards(layer_input, w_up, w_down, parked_codes, parked_scales, parked_rows, incoming):
    core = lax.axis_index("core")
    x = lax.axis_index("x")
    zh = lax.axis_index("zh")
    pos = jnp.stack([core, x, zh]).astype(jnp.int32)

    gap = PACK - OWN
    lines = jnp.stack(
        [
            (parked_rows >> 5).astype(BF16),
            (parked_rows & 31).astype(BF16),
            parked_scales,
        ]
    )
    lines = jnp.tile(jnp.pad(lines, ((0, gap - 3), (0, gap))), (1, 16))
    pack = swap(jnp.concatenate([parked_codes, lines], axis=0), "half")
    pack_far = swap(pack, "core")
    g_far = swap(lax.dynamic_slice(incoming, ((1 - core) * HALF, 0), (HALF, 256)), "core")
    v_far = swap(w_down, "core")
    u_far = swap(w_up, "core")

    scales = pack[OWN + 2, :OWN].astype(F32)
    values = pack[:OWN].astype(F32) * scales[:, None]
    act = jax.nn.gelu(values, approximate=False).astype(BF16)
    act = lax.all_gather(act, ("zb", "y", "core"), tiled=True)

    partial_act = call(
        front, (8, HALF + 2 * PACK, 128), BF16, (pos, incoming, g_far, w_down, v_far, pack, pack_far),
        flops=2 * HALF * 512 * 1024, nbytes=4 << 20,
    )
    recv = lax.all_to_all(partial_act, CHIPS, 0, 0, tiled=True)
    hg = call(slope, (8, HALF, 128), BF16, (pos, recv), flops=1 << 27, nbytes=2 << 20)
    hg = lax.all_to_all(hg, CHIPS, 0, 0, tiled=True)
    hg_far = swap(hg, "core")

    part = call(
        input_part, (HALF, 512), BF16, (pos, hg, w_up, u_far),
        flops=2 * HALF * 512 * 1024, nbytes=3 << 20,
    )
    part = lax.all_to_all(part.reshape(4, 96, 512), "x", 0, 0, tiled=True)
    summed = call(add_x, (96, 512), BF16, (pos, part, incoming, g_far), nbytes=1 << 20)
    got = [
        lax.ppermute(summed, ("half", "zh"), [(4 + i, (i + k) % 4) for i in range(4)])
        for k in range(4)
    ]
    whole = call(add_z, (8, 96, 256), BF16, (pos, *got), nbytes=1 << 20)
    passed = lax.all_to_all(whole, ("core", "x"), 0, 0, tiled=True).reshape(TOK, 256)

    grad_down = call(
        down, (256, 1024), BF16, (pos, recv, incoming, act),
        scratch=(pltpu.VMEM((TOK, 256), BF16),), flops=2 * TOK * 256 * 1792, nbytes=4 << 20,
    )
    grad_up = call(
        up, (256, 1024), BF16, (pos, layer_input, hg, hg_far),
        flops=2 * TOK * 256 * 1024, nbytes=3 << 20,
    )
    return grad_up, grad_down, passed


def solution(mesh):
    fine = Mesh(mesh.devices.reshape(SHAPE), NAMES)
    return jax.shard_map(
        shards,
        mesh=fine,
        in_specs=(
            P(None, SECTION),
            P(SECTION, TENSOR),
            P(SECTION, TENSOR),
            P(SECTION, TENSOR),
            P(SECTION),
            P(SECTION),
            P(None, SECTION),
        ),
        out_specs=(P(SECTION, TENSOR), P(SECTION, TENSOR), P(None, SECTION)),
        check_vma=False,
    )
```

```python
import jax
import jax.numpy as jnp
from jax import lax
from jax.experimental import pallas as pl
from jax.experimental.pallas import tpu as pltpu
from jax.sharding import Mesh, PartitionSpec as P

SHAPE = (2, 2, 4, 2, 4, 4)
NAMES = ("half", "zb", "y", "core", "zh", "x")
SECTION = ("half", "zb", "y", "core")
TENSOR = ("zh", "x")
CHIPS = ("zb", "y")
F32 = jnp.float32
BF16 = jnp.bfloat16
TOK = 768
HALF = 384
OWN = 48
PACK = 64
STACK = 608
VMEM = pl.BlockSpec(memory_space=pltpu.VMEM)
ANY = pl.BlockSpec(memory_space=pl.ANY)
HBM = pl.BlockSpec(memory_space=pltpu.HBM)
DMA = pltpu.SemaphoreType.DMA


def call(kernel, outs, ins, scratch=(), flops=0, nbytes=0, vmem=48, **kwargs):
    many = isinstance(outs, list)
    shapes = [jax.ShapeDtypeStruct(shape, dtype) for shape, dtype in (outs if many else [outs])]
    kwargs.setdefault("in_specs", [VMEM] * len(ins))
    kwargs.setdefault("out_specs", [VMEM] * len(shapes) if many else VMEM)
    return pl.pallas_call(
        kernel,
        out_shape=shapes if many else shapes[0],
        scratch_shapes=list(scratch),
        compiler_params=pltpu.CompilerParams(vmem_limit_bytes=vmem << 20),
        cost_estimate=pl.CostEstimate(flops=flops, bytes_accessed=nbytes, transcendentals=0),
        **kwargs,
    )(*ins)


def swap(value, axis):
    return lax.ppermute(value, axis, [(0, 1), (1, 0)])


def dot(a, b, ca, cb):
    return lax.dot_general(a, b, (((ca,), (cb,)), ((), ())), preferred_element_type=F32)


def run(copies):
    for copy in copies:
        copy.start()
    for copy in copies:
        copy.wait()


def prepare(codes, rows, scales, g, v, u, pack, stack, mine, row_held, scale_held, sems):
    core = lax.axis_index("core")
    near_at, far_at = core * HALF, (1 - core) * HALF
    copies = [
        pltpu.make_async_copy(codes, pack.at[pl.ds(0, OWN), :], sems.at[0]),
        pltpu.make_async_copy(v, stack.at[pl.ds(0, 256), :], sems.at[1]),
        pltpu.make_async_copy(u, stack.at[pl.ds(256, 256), :], sems.at[2]),
        pltpu.make_async_copy(g.at[pl.ds(pl.multiple_of(near_at, HALF), HALF), :], mine, sems.at[3]),
    ]
    for k in range(4):
        copies.append(
            pltpu.make_async_copy(
                g.at[pl.ds(pl.multiple_of(far_at + 96 * k, 96), 96), :],
                stack.at[pl.ds(512, 96), pl.ds(256 * k, 256)],
                sems.at[4 + k],
            )
        )
    lists = [
        pltpu.make_async_copy(rows, row_held, sems.at[8]),
        pltpu.make_async_copy(scales, scale_held, sems.at[9]),
    ]
    for copy in lists + copies:
        copy.start()
    for copy in lists:
        copy.wait()
    row = row_held[...].reshape(1, OWN)
    kind = lax.broadcasted_iota(jnp.int32, (PACK - OWN, 128), 0)

    def spread(line):
        line = jnp.pad(line.astype(F32), ((0, 0), (0, PACK - OWN)))
        return jnp.concatenate([line, line], axis=1)

    high, low, scale = spread(row >> 5), spread(row & 31), spread(scale_held[...].reshape(1, OWN))
    text = jnp.where(kind == 0, high, jnp.where(kind == 1, low, jnp.where(kind == 2, scale, 0.0)))
    text = text.astype(BF16)
    for i in range(8):
        pack[OWN:, 128 * i : 128 * i + 128] = text
    for copy in copies:
        copy.wait()


def front(mine, near, far, out):
    own = mine[...]
    other = jnp.concatenate([far[512:, 256 * k : 256 * k + 256] for k in range(4)], axis=0)
    for j in range(4):
        cols = slice(256 * j, 256 * j + 256)
        part = dot(own, near[:256, cols], 1, 0) + dot(other, far[:256, cols], 1, 0)
        part = part.astype(BF16)
        out[2 * j, :HALF, :] = part[:, :128]
        out[2 * j + 1, :HALF, :] = part[:, 128:]


def attach(pack, _, out, sems):
    run(
        [
            pltpu.make_async_copy(
                pack.at[:, pl.ds(128 * i, 128)], out.at[i, pl.ds(HALF, PACK), :], sems.at[i]
            )
            for i in range(8)
        ]
    )


def add_up(recv, act, packs):
    total = recv[0, :HALF, :].astype(F32)
    for i in range(1, 8):
        total = total + recv[i, :HALF, :].astype(F32)
    act[...] = total
    for i in range(8):
        packs[i] = recv[i, HALF:, :]


def slope(act, near, far, out):
    hidden = jnp.zeros((HALF, 128), F32)
    scale = jnp.zeros((HALF, 128), F32)
    token = lax.broadcasted_iota(jnp.int32, (HALF, 128), 0) + lax.axis_index("core") * HALF
    lane = lax.broadcasted_iota(jnp.int32, (1, 128), 1)
    valid = (lane % PACK) < OWN
    for i in range(8):
        text = jnp.where(
            lane < PACK, near[i, OWN:, :].astype(F32), far[i, OWN:, :].astype(F32)
        )
        rows = (text[0:1] * 32.0 + text[1:2]).astype(jnp.int32)
        hit = (token == rows) & valid
        codes = jnp.concatenate([near[i], far[i]], axis=0)
        hidden = hidden + dot(jnp.where(hit, 1.0, 0.0).astype(BF16), codes, 1, 0)
        scale = scale + jnp.where(hit, text[2:3], 0.0)
    hidden = hidden * jnp.sum(scale, axis=1, keepdims=True)
    density = jnp.exp(-0.5 * hidden * hidden) * 0.3989422804014327
    cumulative = 0.5 * (1.0 + lax.erf(hidden * 0.7071067811865476))
    grad = (act[...] * (cumulative + hidden * density)).astype(BF16)
    activated = (hidden * cumulative).astype(BF16)
    for i in range(8):
        out[i, :HALF, :] = grad
        out[i, HALF:, :] = activated


def input_part(both, near, far, out):
    core = lax.axis_index("core")
    rows = jnp.concatenate([both[i, :HALF, :] for i in range(8)], axis=1)
    near_at = pl.multiple_of(256 * core, 256)
    far_at = pl.multiple_of(256 * (1 - core), 256)
    out[:, pl.ds(near_at, 256)] = dot(rows, near[256:512, :], 1, 1).astype(BF16)
    out[:, pl.ds(far_at, 256)] = dot(rows, far[256:512, :], 1, 1).astype(BF16)


def add_x(recv, mine, far, out):
    core, x = lax.axis_index("core"), lax.axis_index("x")
    total = recv[0].astype(F32)
    for i in range(1, 4):
        total = total + recv[i].astype(F32)
    out[...] = total.astype(BF16)

    @pl.when(lax.axis_index("zh") == 0)
    def _():
        own = mine[pl.ds(pl.multiple_of(x * 96, 96), 96), :].astype(F32)
        other = far[512:, pl.ds(pl.multiple_of(x * 256, 256), 256)].astype(F32)
        left = jnp.where(core == 0, own, other)
        right = jnp.where(core == 0, other, own)
        out[...] = (total + jnp.concatenate([left, right], axis=1)).astype(BF16)


def add_z(_, a, b, c, d, out):
    total = a[...].astype(F32) + b[...].astype(F32) + c[...].astype(F32) + d[...].astype(F32)
    total = total.astype(BF16)
    for i in range(4):
        out[i] = total[:, :256]
        out[4 + i] = total[:, 256:]


def follow(*_):
    pass


def weights(x, g, both, both_far, grad_up, grad_down, after):
    core = lax.axis_index("core")
    after[...] = jnp.zeros_like(after)
    near_at = pl.multiple_of(core * HALF, HALF)
    far_at = pl.multiple_of((1 - core) * HALF, HALF)
    for left, rows, out in ((x, slice(0, HALF), grad_up), (g, slice(HALF, 2 * HALF), grad_down)):
        mine = left[pl.ds(near_at, HALF), :].T
        far = left[pl.ds(far_at, HALF), :].T
        for j in range(4):
            near_cols = jnp.concatenate([both[2 * j, rows, :], both[2 * j + 1, rows, :]], axis=1)
            far_cols = jnp.concatenate([both_far[2 * j, rows, :], both_far[2 * j + 1, rows, :]], axis=1)
            part = dot(mine, near_cols, 1, 0) + dot(far, far_cols, 1, 0)
            out[:, 256 * j : 256 * j + 256] = part.astype(BF16)


def shards(layer_input, w_up, w_down, parked_codes, parked_scales, parked_rows, incoming):
    pack, near, mine = call(
        prepare, [((PACK, 1024), BF16), ((STACK, 1024), BF16), ((HALF, 256), BF16)],
        (parked_codes, parked_rows, parked_scales, incoming, w_down, w_up),
        in_specs=[HBM] * 6, nbytes=5 << 20, vmem=60,
        scratch=(pltpu.VMEM((OWN,), jnp.int32), pltpu.VMEM((OWN,), BF16), DMA((10,))),
    )
    pack = swap(pack, "half")
    far = swap(near, "core")

    wide = HALF + PACK
    sent = call(
        front, ((8, wide, 128), BF16), (mine, near, far)
    )
    sent = call(
        attach, ((8, wide, 128), BF16), (pack, sent), scratch=(DMA((8,)),),
        nbytes=1 << 18, in_specs=[VMEM, ANY], out_specs=ANY, input_output_aliases={1: 0},
    )
    recv = lax.all_to_all(sent, CHIPS, 0, 0, tiled=True)
    act, packs = call(add_up, [((HALF, 128), F32), ((8, PACK, 128), BF16)], (recv,), nbytes=1 << 20)
    packs_far = swap(packs, "core")
    both = call(
        slope, ((8, 2 * HALF, 128), BF16), (act, packs, packs_far), flops=1 << 27, nbytes=2 << 20
    )
    both = lax.all_to_all(both, CHIPS, 0, 0, tiled=True)

    part = call(
        input_part, ((HALF, 512), BF16), (both, near, far),
        flops=2 * HALF * 512 * 1024, nbytes=3 << 20,
    )
    part = lax.all_to_all(part.reshape(4, 96, 512), "x", 0, 0, tiled=True)
    summed = call(add_x, ((96, 512), BF16), (part, mine, far), nbytes=1 << 20)
    got = [
        lax.ppermute(summed, ("half", "zh"), [(4 + i, (i + k) % 4) for i in range(4)])
        for k in range(4)
    ]
    later = call(
        follow, ((8, 2 * HALF, 128), BF16), (part, both), in_specs=[ANY, ANY], out_specs=ANY,
        input_output_aliases={1: 0},
    )
    later_far = swap(later, "core")
    grad_up, grad_down, after = call(
        weights, [((256, 1024), BF16), ((256, 1024), BF16), ((8, 128), F32)],
        (layer_input, incoming, later, later_far), flops=4 * TOK * 256 * 1024, nbytes=5 << 20,
    )
    whole = call(
        add_z, ((8, 96, 256), BF16), (after, *got), nbytes=1 << 20
    )
    passed = lax.all_to_all(whole, ("core", "x"), 0, 0, tiled=True).reshape(TOK, 256)
    return grad_up, grad_down, passed


def solution(mesh):
    fine = Mesh(mesh.devices.reshape(SHAPE), NAMES)
    return jax.shard_map(
        shards,
        mesh=fine,
        in_specs=(
            P(None, SECTION),
            P(SECTION, TENSOR),
            P(SECTION, TENSOR),
            P(SECTION, TENSOR),
            P(SECTION),
            P(SECTION),
            P(None, SECTION),
        ),
        out_specs=(P(SECTION, TENSOR), P(SECTION, TENSOR), P(None, SECTION)),
        check_vma=False,
    )
```

```python
import jax
import jax.numpy as jnp
from jax import lax
from jax.experimental import pallas as pl
from jax.experimental.pallas import tpu as pltpu
from jax.sharding import Mesh, PartitionSpec as P

SHAPE = (2, 2, 4, 2, 4, 4)
NAMES = ("half", "zb", "y", "core", "zh", "x")
SECTION = ("half", "zb", "y", "core")
TENSOR = ("zh", "x")
CHIPS = ("zb", "y")
F32 = jnp.float32
BF16 = jnp.bfloat16
TOK = 768
HALF = 384
OWN = 48
PACK = 64
STACK = 352
VMEM = pl.BlockSpec(memory_space=pltpu.VMEM)
ANY = pl.BlockSpec(memory_space=pl.ANY)
HBM = pl.BlockSpec(memory_space=pltpu.HBM)
DMA = pltpu.SemaphoreType.DMA


def call(kernel, outs, ins, scratch=(), flops=0, nbytes=0, vmem=48, **kwargs):
    many = isinstance(outs, list)
    shapes = [jax.ShapeDtypeStruct(shape, dtype) for shape, dtype in (outs if many else [outs])]
    kwargs.setdefault("in_specs", [VMEM] * len(ins))
    kwargs.setdefault("out_specs", [VMEM] * len(shapes) if many else VMEM)
    return pl.pallas_call(
        kernel,
        out_shape=shapes if many else shapes[0],
        scratch_shapes=list(scratch),
        compiler_params=pltpu.CompilerParams(vmem_limit_bytes=vmem << 20),
        cost_estimate=pl.CostEstimate(flops=flops, bytes_accessed=nbytes, transcendentals=0),
        **kwargs,
    )(*ins)


def swap(value, axis):
    return lax.ppermute(value, axis, [(0, 1), (1, 0)])


def dot(a, b, ca, cb):
    return lax.dot_general(a, b, (((ca,), (cb,)), ((), ())), preferred_element_type=F32)


def prepare(codes, rows, scales, g, v, packs, stack, row_held, scale_held, sems):
    far_at = (1 - lax.axis_index("core")) * HALF
    lists = [
        pltpu.make_async_copy(rows, row_held, sems.at[0]),
        pltpu.make_async_copy(scales, scale_held, sems.at[1]),
    ]
    cut = [
        pltpu.make_async_copy(
            codes.at[:, pl.ds(128 * i, 128)], packs.at[i, pl.ds(0, OWN), :], sems.at[2 + i]
        )
        for i in range(8)
    ]
    bulk = [pltpu.make_async_copy(v, stack.at[pl.ds(0, 256), :], sems.at[10])]
    for k in range(4):
        bulk.append(
            pltpu.make_async_copy(
                g.at[pl.ds(pl.multiple_of(far_at + 96 * k, 96), 96), :],
                stack.at[pl.ds(256, 96), pl.ds(256 * k, 256)],
                sems.at[11 + k],
            )
        )
    for copy in lists + cut + bulk:
        copy.start()
    for copy in lists:
        copy.wait()
    row = row_held[...].reshape(1, OWN)
    kind = lax.broadcasted_iota(jnp.int32, (PACK - OWN, 128), 0)

    def spread(line):
        line = jnp.pad(line.astype(F32), ((0, 0), (0, PACK - OWN)))
        return jnp.concatenate([line, line], axis=1)

    high, low, scale = spread(row >> 5), spread(row & 31), spread(scale_held[...].reshape(1, OWN))
    text = jnp.where(kind == 0, high, jnp.where(kind == 1, low, jnp.where(kind == 2, scale, 0.0)))
    text = text.astype(BF16)
    for i in range(16):
        packs[i, OWN:, :] = text
    for i in range(8):
        cut[i].wait()
        packs[8 + i, :OWN, :] = packs[i, :OWN, :]
    for copy in bulk:
        copy.wait()


def front(g, v, far, out, g_held, v_held, far_held, sems):
    near_at = pl.multiple_of(lax.axis_index("core") * HALF, HALF)
    copies = [
        pltpu.make_async_copy(g.at[pl.ds(near_at, HALF), :], g_held, sems.at[0]),
        pltpu.make_async_copy(v, v_held, sems.at[1]),
        pltpu.make_async_copy(far, far_held, sems.at[2]),
    ]
    for copy in copies:
        copy.start()
    for copy in copies:
        copy.wait()
    own = g_held[...]
    other = jnp.concatenate([far_held[256:, 256 * k : 256 * k + 256] for k in range(4)], axis=0)
    for j in range(4):
        cols = slice(256 * j, 256 * j + 256)
        part = dot(own, v_held[:, cols], 1, 0) + dot(other, far_held[:256, cols], 1, 0)
        part = part.astype(BF16)
        out[2 * j] = part[:, :128]
        out[2 * j + 1] = part[:, 128:]


def slope(recv, near, far, _, grads, activations):
    act = recv[0].astype(F32)
    for i in range(1, 8):
        act = act + recv[i].astype(F32)
    hidden = jnp.zeros((HALF, 128), F32)
    scale = jnp.zeros((HALF, 128), F32)
    token = lax.broadcasted_iota(jnp.int32, (HALF, 128), 0) + lax.axis_index("core") * HALF
    lane = lax.broadcasted_iota(jnp.int32, (1, 128), 1)
    valid = (lane % PACK) < OWN
    mirror = 8 * (1 - lax.axis_index("half"))
    for i in range(8):
        one, two = near[mirror + i], far[mirror + i]
        text = jnp.where(lane < PACK, one[OWN:].astype(F32), two[OWN:].astype(F32))
        rows = (text[0:1] * 32.0 + text[1:2]).astype(jnp.int32)
        hit = (token == rows) & valid
        codes = jnp.concatenate([one, two], axis=0)
        hidden = hidden + dot(jnp.where(hit, 1.0, 0.0).astype(BF16), codes, 1, 0)
        scale = scale + jnp.where(hit, text[2:3], 0.0)
    hidden = hidden * jnp.sum(scale, axis=1, keepdims=True)
    density = jnp.exp(-0.5 * hidden * hidden) * 0.3989422804014327
    cumulative = 0.5 * (1.0 + lax.erf(hidden * 0.7071067811865476))
    grad = (act * (cumulative + hidden * density)).astype(BF16)
    activated = (hidden * cumulative).astype(BF16)
    for i in range(8):
        grads[i] = grad
        activations[i] = activated


def input_part(hg, near, far, out):
    core = lax.axis_index("core")
    rows = jnp.concatenate([hg[i] for i in range(8)], axis=1)
    near_at = pl.multiple_of(256 * core, 256)
    far_at = pl.multiple_of(256 * (1 - core), 256)
    out[:, pl.ds(near_at, 256)] = dot(rows, near[...], 1, 1).astype(BF16)
    out[:, pl.ds(far_at, 256)] = dot(rows, far[...], 1, 1).astype(BF16)


def add_x(recv, g, far, out):
    core, x = lax.axis_index("core"), lax.axis_index("x")
    total = recv[0].astype(F32)
    for i in range(1, 4):
        total = total + recv[i].astype(F32)
    out[...] = total.astype(BF16)

    @pl.when(lax.axis_index("zh") == 0)
    def _():
        own = g[pl.ds(pl.multiple_of(core * HALF + x * 96, 96), 96), :].astype(F32)
        other = far[256:, pl.ds(pl.multiple_of(x * 256, 256), 256)].astype(F32)
        left = jnp.where(core == 0, own, other)
        right = jnp.where(core == 0, other, own)
        out[...] = (total + jnp.concatenate([left, right], axis=1)).astype(BF16)


def add_z(a, b, c, d, out):
    total = a[...].astype(F32) + b[...].astype(F32) + c[...].astype(F32) + d[...].astype(F32)
    total = total.astype(BF16)
    for i in range(4):
        out[i] = total[:, :256]
        out[4 + i] = total[:, 256:]


def finish(blocks, _, __, out):
    for i in range(8):
        out[96 * i : 96 * i + 96, :] = blocks[i]


def follow(*_):
    pass


def weights(left, near, far, out, after):
    after[...] = jnp.zeros_like(after)
    core = lax.axis_index("core")
    mine = left[pl.ds(pl.multiple_of(core * HALF, HALF), HALF), :].T
    other = left[pl.ds(pl.multiple_of((1 - core) * HALF, HALF), HALF), :].T
    for j in range(4):
        near_cols = jnp.concatenate([near[2 * j], near[2 * j + 1]], axis=1)
        far_cols = jnp.concatenate([far[2 * j], far[2 * j + 1]], axis=1)
        part = dot(mine, near_cols, 1, 0) + dot(other, far_cols, 1, 0)
        out[:, 256 * j : 256 * j + 256] = part.astype(BF16)


def shards(layer_input, w_up, w_down, parked_codes, parked_scales, parked_rows, incoming):
    packs, near = call(
        prepare, [((16, PACK, 128), BF16), ((STACK, 1024), BF16)],
        (parked_codes, parked_rows, parked_scales, incoming, w_down), in_specs=[HBM] * 5, nbytes=3 << 20,
        vmem=60, scratch=(pltpu.VMEM((OWN,), jnp.int32), pltpu.VMEM((OWN,), BF16), DMA((15,))),
    )
    packs = lax.all_to_all(packs, ("half",) + CHIPS, 0, 0, tiled=True)
    packs_far = swap(packs, "core")
    far = swap(near, "core")
    u_far = swap(w_up, "core")

    sent = call(
        front, ((8, HALF, 128), BF16), (incoming, w_down, far), in_specs=[HBM] * 3, vmem=60,
        scratch=(
            pltpu.VMEM((HALF, 256), BF16), pltpu.VMEM((256, 1024), BF16),
            pltpu.VMEM((STACK, 1024), BF16), DMA((3,)),
        ),
    )
    recv = lax.all_to_all(sent, CHIPS, 0, 0, tiled=True)
    share = ((8, HALF, 128), BF16)
    hg, act = call(
        slope, [share, share], (recv, packs, packs_far, u_far), flops=1 << 27, nbytes=2 << 20,
        in_specs=[VMEM] * 3 + [ANY],
    )
    hg = lax.all_to_all(hg, CHIPS, 0, 0, tiled=True)

    part = call(
        input_part, ((HALF, 512), BF16), (hg, w_up, u_far),
        flops=2 * HALF * 512 * 1024, nbytes=3 << 20,
    )
    hg = call(follow, share, (part, hg), in_specs=[ANY, ANY], out_specs=ANY, input_output_aliases={1: 0})
    hg_far = swap(hg, "core")
    part = lax.all_to_all(part.reshape(4, 96, 512), "x", 0, 0, tiled=True)
    summed = call(add_x, ((96, 512), BF16), (part, incoming, far), nbytes=1 << 20)
    got = [
        lax.ppermute(summed, ("half", "zh"), [(4 + i, (i + k) % 4) for i in range(4)])
        for k in range(4)
    ]
    act = call(follow, share, (summed, act), in_specs=[ANY, ANY], out_specs=ANY, input_output_aliases={1: 0}, nbytes=64 << 20)
    act = lax.all_to_all(act, CHIPS, 0, 0, tiled=True)
    whole = call(add_z, ((8, 96, 256), BF16), got)
    whole, act = call(
        follow, [((8, 96, 256), BF16), share], (whole, act), in_specs=[ANY] * 2, out_specs=[ANY] * 2,
        input_output_aliases={0: 0, 1: 1},
    )
    passed = lax.all_to_all(whole, ("core", "x"), 0, 0, tiled=True)
    (grad_up, up), (grad_down, down) = [
        call(
            weights, [((256, 1024), BF16), ((8, 128), F32)], (left, near, far),
            flops=2 * TOK * 256 * 1024, nbytes=3 << 20,
        )
        for left, near, far in ((layer_input, hg, hg_far), (incoming, act, swap(act, "core")))
    ]
    passed = call(finish, ((TOK, 256), BF16), (passed, up, down))
    return grad_up, grad_down, passed


def solution(mesh):
    fine = Mesh(mesh.devices.reshape(SHAPE), NAMES)
    return jax.shard_map(
        shards,
        mesh=fine,
        in_specs=(
            P(None, SECTION),
            P(SECTION, TENSOR),
            P(SECTION, TENSOR),
            P(SECTION, TENSOR),
            P(SECTION),
            P(SECTION),
            P(None, SECTION),
        ),
        out_specs=(P(SECTION, TENSOR), P(SECTION, TENSOR), P(None, SECTION)),
        check_vma=False,
    )
```

```python
import jax
import jax.numpy as jnp
from jax import lax
from jax.experimental import pallas as pl
from jax.experimental.pallas import tpu as pltpu
from jax.sharding import Mesh, PartitionSpec as P

SHAPE = (2, 2, 4, 2, 4, 4)
NAMES = ("half", "zb", "y", "core", "zh", "x")
SECTION = ("half", "zb", "y", "core")
TENSOR = ("zh", "x")
CHIPS = ("zb", "y")
F32 = jnp.float32
BF16 = jnp.bfloat16
TOK = 768
HALF = 384
OWN = 48
PACK = 64
STACK = 352
VMEM = pl.BlockSpec(memory_space=pltpu.VMEM)
ANY = pl.BlockSpec(memory_space=pl.ANY)
HBM = pl.BlockSpec(memory_space=pltpu.HBM)
DMA = pltpu.SemaphoreType.DMA


def call(kernel, outs, ins, scratch=(), flops=0, nbytes=0, vmem=48, **kwargs):
    many = isinstance(outs, list)
    shapes = [jax.ShapeDtypeStruct(shape, dtype) for shape, dtype in (outs if many else [outs])]
    kwargs.setdefault("in_specs", [VMEM] * len(ins))
    kwargs.setdefault("out_specs", [VMEM] * len(shapes) if many else VMEM)
    return pl.pallas_call(
        kernel,
        out_shape=shapes if many else shapes[0],
        scratch_shapes=list(scratch),
        compiler_params=pltpu.CompilerParams(vmem_limit_bytes=vmem << 20),
        cost_estimate=pl.CostEstimate(flops=flops, bytes_accessed=nbytes, transcendentals=0),
        **kwargs,
    )(*ins)


def swap(value, axis):
    return lax.ppermute(value, axis, [(0, 1), (1, 0)])


def dot(a, b, ca, cb):
    return lax.dot_general(a, b, (((ca,), (cb,)), ((), ())), preferred_element_type=F32)


def prepare(codes, rows, scales, g, v, packs, stack, row_held, scale_held, sems):
    far_at = (1 - lax.axis_index("core")) * HALF
    lists = [
        pltpu.make_async_copy(rows, row_held, sems.at[0]),
        pltpu.make_async_copy(scales, scale_held, sems.at[1]),
    ]
    cut = [
        pltpu.make_async_copy(
            codes.at[:, pl.ds(128 * i, 128)], packs.at[i, pl.ds(0, OWN), :], sems.at[2 + i]
        )
        for i in range(8)
    ]
    bulk = [pltpu.make_async_copy(v, stack.at[pl.ds(0, 256), :], sems.at[10])]
    for k in range(4):
        bulk.append(
            pltpu.make_async_copy(
                g.at[pl.ds(pl.multiple_of(far_at + 96 * k, 96), 96), :],
                stack.at[pl.ds(256, 96), pl.ds(256 * k, 256)],
                sems.at[11 + k],
            )
        )
    for copy in lists + cut + bulk:
        copy.start()
    for copy in lists:
        copy.wait()
    row = row_held[...].reshape(1, OWN)
    kind = lax.broadcasted_iota(jnp.int32, (PACK - OWN, 128), 0)

    def spread(line):
        line = jnp.pad(line.astype(F32), ((0, 0), (0, PACK - OWN)))
        return jnp.concatenate([line, line], axis=1)

    high, low, scale = spread(row >> 5), spread(row & 31), spread(scale_held[...].reshape(1, OWN))
    text = jnp.where(kind == 0, high, jnp.where(kind == 1, low, jnp.where(kind == 2, scale, 0.0)))
    text = text.astype(BF16)
    for i in range(16):
        packs[i, OWN:, :] = text
    for i in range(8):
        cut[i].wait()
        packs[8 + i, :OWN, :] = packs[i, :OWN, :]
    for copy in bulk:
        copy.wait()


def front(g, v, far, out, g_held, v_held, far_held, sems):
    near_at = pl.multiple_of(lax.axis_index("core") * HALF, HALF)
    copies = [
        pltpu.make_async_copy(g.at[pl.ds(near_at, HALF), :], g_held, sems.at[0]),
        pltpu.make_async_copy(v, v_held, sems.at[1]),
        pltpu.make_async_copy(far, far_held, sems.at[2]),
    ]
    for copy in copies:
        copy.start()
    for copy in copies:
        copy.wait()
    own = g_held[...]
    other = jnp.concatenate([far_held[256:, 256 * k : 256 * k + 256] for k in range(4)], axis=0)
    for j in range(4):
        cols = slice(256 * j, 256 * j + 256)
        part = dot(own, v_held[:, cols], 1, 0) + dot(other, far_held[:256, cols], 1, 0)
        part = part.astype(BF16)
        out[2 * j] = part[:, :128]
        out[2 * j + 1] = part[:, 128:]


def slope(recv, near, far, _, grads, activations):
    act = recv[0].astype(F32)
    for i in range(1, 8):
        act = act + recv[i].astype(F32)
    hidden = jnp.zeros((HALF, 128), F32)
    scale = jnp.zeros((HALF, 128), F32)
    token = lax.broadcasted_iota(jnp.int32, (HALF, 128), 0) + lax.axis_index("core") * HALF
    lane = lax.broadcasted_iota(jnp.int32, (1, 128), 1)
    valid = (lane % PACK) < OWN
    mirror = 8 * (1 - lax.axis_index("half"))
    for i in range(8):
        one, two = near[mirror + i], far[mirror + i]
        text = jnp.where(lane < PACK, one[OWN:].astype(F32), two[OWN:].astype(F32))
        rows = (text[0:1] * 32.0 + text[1:2]).astype(jnp.int32)
        hit = (token == rows) & valid
        codes = jnp.concatenate([one, two], axis=0)
        hidden = hidden + dot(jnp.where(hit, 1.0, 0.0).astype(BF16), codes, 1, 0)
        scale = scale + jnp.where(hit, text[2:3], 0.0)
    hidden = hidden * jnp.sum(scale, axis=1, keepdims=True)
    density = jnp.exp(-0.5 * hidden * hidden) * 0.3989422804014327
    cumulative = 0.5 * (1.0 + lax.erf(hidden * 0.7071067811865476))
    grad = (act * (cumulative + hidden * density)).astype(BF16)
    activated = (hidden * cumulative).astype(BF16)
    for i in range(8):
        grads[i] = grad
        activations[i] = activated


def input_part(hg, near, far, out):
    core = lax.axis_index("core")
    rows = jnp.concatenate([hg[i] for i in range(8)], axis=1)
    near_at = pl.multiple_of(256 * core, 256)
    far_at = pl.multiple_of(256 * (1 - core), 256)
    out[:, pl.ds(near_at, 256)] = dot(rows, near[...], 1, 1).astype(BF16)
    out[:, pl.ds(far_at, 256)] = dot(rows, far[...], 1, 1).astype(BF16)


def add_x(recv, g, far, out):
    core, x = lax.axis_index("core"), lax.axis_index("x")
    total = recv[0].astype(F32)
    for i in range(1, 4):
        total = total + recv[i].astype(F32)
    out[...] = total.astype(BF16)

    @pl.when(lax.axis_index("zh") == 0)
    def _():
        own = g[pl.ds(pl.multiple_of(core * HALF + x * 96, 96), 96), :].astype(F32)
        other = far[256:, pl.ds(pl.multiple_of(x * 256, 256), 256)].astype(F32)
        left = jnp.where(core == 0, own, other)
        right = jnp.where(core == 0, other, own)
        out[...] = (total + jnp.concatenate([left, right], axis=1)).astype(BF16)


def add_z(_, __, a, b, c, d, out):
    total = a[...].astype(F32) + b[...].astype(F32) + c[...].astype(F32) + d[...].astype(F32)
    total = total.astype(BF16)
    for i in range(4):
        out[i] = total[:, :256]
        out[4 + i] = total[:, 256:]


def finish(blocks, out):
    for i in range(8):
        out[96 * i : 96 * i + 96, :] = blocks[i]


def follow(*_):
    pass


def weights(left, near, far, out, after):
    after[...] = jnp.zeros_like(after)
    core = lax.axis_index("core")
    mine = left[pl.ds(pl.multiple_of(core * HALF, HALF), HALF), :].T
    other = left[pl.ds(pl.multiple_of((1 - core) * HALF, HALF), HALF), :].T
    for j in range(4):
        near_cols = jnp.concatenate([near[2 * j], near[2 * j + 1]], axis=1)
        far_cols = jnp.concatenate([far[2 * j], far[2 * j + 1]], axis=1)
        part = dot(mine, near_cols, 1, 0) + dot(other, far_cols, 1, 0)
        out[:, 256 * j : 256 * j + 256] = part.astype(BF16)


def shards(layer_input, w_up, w_down, parked_codes, parked_scales, parked_rows, incoming):
    packs, near = call(
        prepare, [((16, PACK, 128), BF16), ((STACK, 1024), BF16)],
        (parked_codes, parked_rows, parked_scales, incoming, w_down), in_specs=[HBM] * 5, nbytes=3 << 20,
        vmem=60, scratch=(pltpu.VMEM((OWN,), jnp.int32), pltpu.VMEM((OWN,), BF16), DMA((15,))),
    )
    packs = lax.all_to_all(packs, ("half",) + CHIPS, 0, 0, tiled=True)
    packs_far = swap(packs, "core")
    far = swap(near, "core")
    u_far = swap(w_up, "core")

    sent = call(
        front, ((8, HALF, 128), BF16), (incoming, w_down, far), in_specs=[HBM] * 3, vmem=60,
        scratch=(
            pltpu.VMEM((HALF, 256), BF16), pltpu.VMEM((256, 1024), BF16),
            pltpu.VMEM((STACK, 1024), BF16), DMA((3,)),
        ),
    )
    recv = lax.all_to_all(sent, CHIPS, 0, 0, tiled=True)
    share = ((8, HALF, 128), BF16)
    hg, act = call(
        slope, [share, share], (recv, packs, packs_far, u_far), flops=1 << 27, nbytes=2 << 20,
        in_specs=[VMEM] * 3 + [ANY],
    )
    hg = lax.all_to_all(hg, CHIPS, 0, 0, tiled=True)

    second = lax.axis_index("half") == 1

    def reduce_x(hg, u, u_far, g, far):
        part = call(
            input_part, ((HALF, 512), BF16), (hg, u, u_far),
            flops=2 * HALF * 512 * 1024, nbytes=3 << 20,
        )
        part = lax.all_to_all(part.reshape(4, 96, 512), "x", 0, 0, tiled=True)
        return call(add_x, ((96, 512), BF16), (part, g, far), nbytes=1 << 20)

    summed = lax.cond(
        second, reduce_x, lambda *_: jnp.zeros((96, 512), BF16), hg, w_up, u_far, incoming, far
    )
    got = [
        lax.ppermute(summed, ("half", "zh"), [(4 + i, (i + k) % 4) for i in range(4)])
        for k in range(4)
    ]

    def gradients(hg, act, x, g):
        act = lax.all_to_all(act, CHIPS, 0, 0, tiled=True)
        def gradient(left, near):
            return call(
                weights, [((256, 1024), BF16), ((8, 128), F32)], (left, near, swap(near, "core")),
                flops=2 * TOK * 256 * 1024, nbytes=3 << 20,
            )

        up, first = gradient(x, hg)
        act = call(follow, share, (first, act), in_specs=[ANY, ANY], out_specs=ANY, input_output_aliases={1: 0})
        down, last = gradient(g, act)
        return up, down, first, last

    def gradients_first(*operands):
        return gradients(*operands)

    grad_up, grad_down, *after = lax.cond(
        second, gradients, gradients_first, hg, act, layer_input, incoming
    )
    whole = call(add_z, ((8, 96, 256), BF16), (*after, *got))

    def spread_x(whole):
        return call(finish, ((TOK, 256), BF16), (lax.all_to_all(whole, ("core", "x"), 0, 0, tiled=True),))

    passed = lax.cond(second, lambda _: jnp.zeros((TOK, 256), BF16), spread_x, whole)
    return grad_up, grad_down, passed


def solution(mesh):
    fine = Mesh(mesh.devices.reshape(SHAPE), NAMES)
    return jax.shard_map(
        shards,
        mesh=fine,
        in_specs=(
            P(None, SECTION),
            P(SECTION, TENSOR),
            P(SECTION, TENSOR),
            P(SECTION, TENSOR),
            P(SECTION),
            P(SECTION),
            P(None, SECTION),
        ),
        out_specs=(P(SECTION, TENSOR), P(SECTION, TENSOR), P(None, SECTION)),
        check_vma=False,
    )
```

```python
import jax
import jax.numpy as jnp
from jax import lax
from jax.experimental import pallas as pl
from jax.experimental.pallas import tpu as pltpu
from jax.sharding import Mesh, PartitionSpec as P

SHAPE = (2, 2, 4, 2, 4, 4)
NAMES = ("half", "zb", "y", "core", "zh", "x")
SECTION = ("half", "zb", "y", "core")
TENSOR = ("zh", "x")
CHIPS = ("zb", "y")
F32 = jnp.float32
BF16 = jnp.bfloat16
TOK = 768
HALF = 384
OWN = 48
PACK = 64
STACK = 352
VMEM = pl.BlockSpec(memory_space=pltpu.VMEM)
ANY = pl.BlockSpec(memory_space=pl.ANY)
HBM = pl.BlockSpec(memory_space=pltpu.HBM)
DMA = pltpu.SemaphoreType.DMA


def call(kernel, outs, ins, scratch=(), flops=0, nbytes=0, vmem=48, **kwargs):
    many = isinstance(outs, list)
    shapes = [jax.ShapeDtypeStruct(shape, dtype) for shape, dtype in (outs if many else [outs])]
    kwargs.setdefault("in_specs", [VMEM] * len(ins))
    kwargs.setdefault("out_specs", [VMEM] * len(shapes) if many else VMEM)
    return pl.pallas_call(
        kernel,
        out_shape=shapes if many else shapes[0],
        scratch_shapes=list(scratch),
        compiler_params=pltpu.CompilerParams(vmem_limit_bytes=vmem << 20),
        cost_estimate=pl.CostEstimate(flops=flops, bytes_accessed=nbytes, transcendentals=0),
        **kwargs,
    )(*ins)


def swap(value, axis):
    return lax.ppermute(value, axis, [(0, 1), (1, 0)])


def dot(a, b, ca, cb):
    return lax.dot_general(a, b, (((ca,), (cb,)), ((), ())), preferred_element_type=F32)


def prepare(codes, rows, scales, g, v, packs, stack, row_held, scale_held, sems):
    far_at = (1 - lax.axis_index("core")) * HALF
    lists = [
        pltpu.make_async_copy(rows, row_held, sems.at[0]),
        pltpu.make_async_copy(scales, scale_held, sems.at[1]),
    ]
    cut = [
        pltpu.make_async_copy(
            codes.at[:, pl.ds(128 * i, 128)], packs.at[i, pl.ds(0, OWN), :], sems.at[2 + i]
        )
        for i in range(8)
    ]
    bulk = [pltpu.make_async_copy(v, stack.at[pl.ds(0, 256), :], sems.at[10])]
    for k in range(4):
        bulk.append(
            pltpu.make_async_copy(
                g.at[pl.ds(pl.multiple_of(far_at + 96 * k, 96), 96), :],
                stack.at[pl.ds(256, 96), pl.ds(256 * k, 256)],
                sems.at[11 + k],
            )
        )
    for copy in lists + cut + bulk:
        copy.start()
    for copy in lists:
        copy.wait()
    row = row_held[...].reshape(1, OWN)
    kind = lax.broadcasted_iota(jnp.int32, (PACK - OWN, 128), 0)

    def spread(line):
        line = jnp.pad(line.astype(F32), ((0, 0), (0, PACK - OWN)))
        return jnp.concatenate([line, line], axis=1)

    high, low, scale = spread(row >> 5), spread(row & 31), spread(scale_held[...].reshape(1, OWN))
    text = jnp.where(kind == 0, high, jnp.where(kind == 1, low, jnp.where(kind == 2, scale, 0.0)))
    text = text.astype(BF16)
    for i in range(16):
        packs[i, OWN:, :] = text
    for i in range(8):
        cut[i].wait()
        packs[8 + i, :OWN, :] = packs[i, :OWN, :]
    for copy in bulk:
        copy.wait()


def keep(_, g, v, mine, v_kept):
    mine[...] = g[pl.ds(pl.multiple_of(lax.axis_index("core") * HALF, HALF), HALF), :]
    v_kept[...] = v[...]


def front(g, v, far, out):
    own = g[...]
    other = jnp.concatenate([far[256:, 256 * k : 256 * k + 256] for k in range(4)], axis=0)
    for j in range(4):
        cols = slice(256 * j, 256 * j + 256)
        part = dot(own, v[:, cols], 1, 0) + dot(other, far[:256, cols], 1, 0)
        part = part.astype(BF16)
        out[2 * j] = part[:, :128]
        out[2 * j + 1] = part[:, 128:]


def slope(recv, near, far, *outs):
    act = recv[0].astype(F32)
    for i in range(1, 8):
        act = act + recv[i].astype(F32)
    hidden = jnp.zeros((HALF, 128), F32)
    scale = jnp.zeros((HALF, 128), F32)
    token = lax.broadcasted_iota(jnp.int32, (HALF, 128), 0) + lax.axis_index("core") * HALF
    lane = lax.broadcasted_iota(jnp.int32, (1, 128), 1)
    valid = (lane % PACK) < OWN
    mirror = 8 * (1 - lax.axis_index("half"))
    for i in range(8):
        one, two = near[mirror + i], far[mirror + i]
        text = jnp.where(lane < PACK, one[OWN:].astype(F32), two[OWN:].astype(F32))
        rows = (text[0:1] * 32.0 + text[1:2]).astype(jnp.int32)
        hit = (token == rows) & valid
        codes = jnp.concatenate([one, two], axis=0)
        hidden = hidden + dot(jnp.where(hit, 1.0, 0.0).astype(BF16), codes, 1, 0)
        scale = scale + jnp.where(hit, text[2:3], 0.0)
    hidden = hidden * jnp.sum(scale, axis=1, keepdims=True)
    density = jnp.exp(-0.5 * hidden * hidden) * 0.3989422804014327
    cumulative = 0.5 * (1.0 + lax.erf(hidden * 0.7071067811865476))
    grad = (act * (cumulative + hidden * density)).astype(BF16)
    activated = (hidden * cumulative).astype(BF16)
    for i in range(8):
        outs[0][i, :HALF, :] = grad
        outs[-1][i, -HALF:, :] = activated


def input_part(hg, near, far, out):
    core = lax.axis_index("core")
    rows = jnp.concatenate([hg[i] for i in range(8)], axis=1)
    near_at = pl.multiple_of(256 * core, 256)
    far_at = pl.multiple_of(256 * (1 - core), 256)
    out[:, pl.ds(near_at, 256)] = dot(rows, near[...], 1, 1).astype(BF16)
    out[:, pl.ds(far_at, 256)] = dot(rows, far[...], 1, 1).astype(BF16)


def add_x(recv, mine, far, out):
    core, x = lax.axis_index("core"), lax.axis_index("x")
    total = recv[0].astype(F32)
    for i in range(1, 4):
        total = total + recv[i].astype(F32)
    out[...] = total.astype(BF16)

    @pl.when(lax.axis_index("zh") == 0)
    def _():
        own = mine[pl.ds(pl.multiple_of(x * 96, 96), 96), :].astype(F32)
        other = far[256:, pl.ds(pl.multiple_of(x * 256, 256), 256)].astype(F32)
        left = jnp.where(core == 0, own, other)
        right = jnp.where(core == 0, other, own)
        out[...] = (total + jnp.concatenate([left, right], axis=1)).astype(BF16)


def add_z(_, __, a, b, c, d, out):
    total = a[...].astype(F32) + b[...].astype(F32) + c[...].astype(F32) + d[...].astype(F32)
    total = total.astype(BF16)
    for i in range(4):
        out[i] = total[:, :256]
        out[4 + i] = total[:, 256:]


def split(both, first, last):
    first[...] = both[:, :HALF, :]
    last[...] = both[:, HALF:, :]


def finish(blocks, out):
    for i in range(8):
        out[96 * i : 96 * i + 96, :] = blocks[i]


def follow(*_):
    pass


def weights(left, near, far, out, after):
    after[...] = jnp.zeros_like(after)
    core = lax.axis_index("core")
    mine = left[pl.ds(pl.multiple_of(core * HALF, HALF), HALF), :].T
    other = left[pl.ds(pl.multiple_of((1 - core) * HALF, HALF), HALF), :].T
    for j in range(4):
        near_cols = jnp.concatenate([near[2 * j], near[2 * j + 1]], axis=1)
        far_cols = jnp.concatenate([far[2 * j], far[2 * j + 1]], axis=1)
        part = dot(mine, near_cols, 1, 0) + dot(other, far_cols, 1, 0)
        out[:, 256 * j : 256 * j + 256] = part.astype(BF16)


def shards(layer_input, w_up, w_down, parked_codes, parked_scales, parked_rows, incoming):
    packs, near = call(
        prepare, [((16, PACK, 128), BF16), ((STACK, 1024), BF16)],
        (parked_codes, parked_rows, parked_scales, incoming, w_down), in_specs=[HBM] * 5, nbytes=3 << 20,
        vmem=60, scratch=(pltpu.VMEM((OWN,), jnp.int32), pltpu.VMEM((OWN,), BF16), DMA((15,))),
    )
    ready = packs
    packs = lax.all_to_all(packs, ("half",) + CHIPS, 0, 0, tiled=True)
    packs_far = swap(packs, "core")
    far = swap(near, "core")
    u_far = swap(w_up, "core")

    mine, v = call(
        keep, [((HALF, 256), BF16), ((256, 1024), BF16)], (ready, incoming, w_down), vmem=24,
        in_specs=[ANY] + [VMEM] * 2,
    )
    sent = call(front, ((8, HALF, 128), BF16), (mine, v, far), vmem=24)
    recv = lax.all_to_all(sent, CHIPS, 0, 0, tiled=True)
    share = ((8, HALF, 128), BF16)
    wide = ((256, 1024), BF16)
    second = lax.axis_index("half") == 1

    def to_x(recv, packs, packs_far, u, u_far):
        hg, act = call(slope, [share, share], (recv, packs, packs_far), flops=1 << 27, nbytes=2 << 20)
        hg = lax.all_to_all(hg, CHIPS, 0, 0, tiled=True)
        part = call(
            input_part, ((HALF, 512), BF16), (hg, u, u_far),
            flops=2 * HALF * 512 * 1024, nbytes=3 << 20,
        )
        return lax.all_to_all(part.reshape(4, 96, 512), "x", 0, 0, tiled=True), hg, act

    def gather_both(recv, packs, packs_far, *_):
        both = call(
            slope, [((8, 2 * HALF, 128), BF16)], (recv, packs, packs_far), flops=1 << 27, nbytes=2 << 20
        )[0]
        both = lax.all_to_all(both, CHIPS, 0, 0, tiled=True)
        hg, act = call(split, [share, share], (both,))
        return jnp.zeros((4, 96, 512), BF16), hg, act

    part, hg, act = lax.cond(second, to_x, gather_both, recv, packs, packs_far, w_up, u_far)
    summed = call(add_x, ((96, 512), BF16), (part, mine, far), nbytes=1 << 20)
    got = [
        lax.ppermute(summed, ("half", "zh"), [(4 + i, (i + k) % 4) for i in range(4)])
        for k in range(4)
    ]

    def gradient(left, near):
        return call(
            weights, [wide, ((8, 128), F32)], (left, near, swap(near, "core")),
            flops=2 * TOK * 256 * 1024, nbytes=3 << 20,
        )

    def gradients(hg, act, x, g):
        up, first = gradient(x, hg)
        act = call(follow, share, (first, act), in_specs=[ANY, ANY], out_specs=ANY, input_output_aliases={1: 0})
        down, last = gradient(g, act)
        return up, down, first, last

    def gather_first(hg, act, x, g):
        return gradients(hg, lax.all_to_all(act, CHIPS, 0, 0, tiled=True), x, g)

    grad_up, grad_down, *after = lax.cond(second, gather_first, gradients, hg, act, layer_input, incoming)
    whole = call(add_z, ((8, 96, 256), BF16), (*after, *got))

    def spread_x(whole):
        return call(finish, ((TOK, 256), BF16), (lax.all_to_all(whole, ("core", "x"), 0, 0, tiled=True),))

    passed = lax.cond(second, lambda _: jnp.zeros((TOK, 256), BF16), spread_x, whole)
    return grad_up, grad_down, passed


def solution(mesh):
    fine = Mesh(mesh.devices.reshape(SHAPE), NAMES)
    return jax.shard_map(
        shards,
        mesh=fine,
        in_specs=(
            P(None, SECTION),
            P(SECTION, TENSOR),
            P(SECTION, TENSOR),
            P(SECTION, TENSOR),
            P(SECTION),
            P(SECTION),
            P(None, SECTION),
        ),
        out_specs=(P(SECTION, TENSOR), P(SECTION, TENSOR), P(None, SECTION)),
        check_vma=False,
    )
```

```python
import jax
import jax.numpy as jnp
from jax import lax
from jax.experimental import pallas as pl
from jax.experimental.pallas import tpu as pltpu
from jax.sharding import Mesh, PartitionSpec as P

SHAPE = (2, 2, 4, 2, 4, 4)
NAMES = ("half", "zb", "y", "core", "zh", "x")
SECTION = ("half", "zb", "y", "core")
TENSOR = ("zh", "x")
CHIPS = ("zb", "y")
F32 = jnp.float32
BF16 = jnp.bfloat16
TOK = 768
HALF = 384
OWN = 48
PACK = 64
STACK = 352
VMEM = pl.BlockSpec(memory_space=pltpu.VMEM)
ANY = pl.BlockSpec(memory_space=pl.ANY)
HBM = pl.BlockSpec(memory_space=pltpu.HBM)
DMA = pltpu.SemaphoreType.DMA


def call(kernel, outs, ins, scratch=(), flops=0, nbytes=0, vmem=48, **kwargs):
    many = isinstance(outs, list)
    shapes = [jax.ShapeDtypeStruct(shape, dtype) for shape, dtype in (outs if many else [outs])]
    kwargs.setdefault("in_specs", [VMEM] * len(ins))
    kwargs.setdefault("out_specs", [VMEM] * len(shapes) if many else VMEM)
    return pl.pallas_call(
        kernel,
        out_shape=shapes if many else shapes[0],
        scratch_shapes=list(scratch),
        compiler_params=pltpu.CompilerParams(vmem_limit_bytes=vmem << 20),
        cost_estimate=pl.CostEstimate(flops=flops, bytes_accessed=nbytes, transcendentals=0),
        **kwargs,
    )(*ins)


def swap(value, axis):
    return lax.ppermute(value, axis, [(0, 1), (1, 0)])


def dot(a, b, ca, cb):
    return lax.dot_general(a, b, (((ca,), (cb,)), ((), ())), preferred_element_type=F32)


def prepare(codes, rows, scales, g, v, packs, stack, row_held, scale_held, sems):
    far_at = (1 - lax.axis_index("core")) * HALF
    lists = [
        pltpu.make_async_copy(rows, row_held, sems.at[0]),
        pltpu.make_async_copy(scales, scale_held, sems.at[1]),
    ]
    cut = [
        pltpu.make_async_copy(
            codes.at[:, pl.ds(128 * i, 128)], packs.at[i, pl.ds(0, OWN), :], sems.at[2 + i]
        )
        for i in range(8)
    ]
    bulk = [pltpu.make_async_copy(v, stack.at[pl.ds(0, 256), :], sems.at[10])]
    for k in range(4):
        bulk.append(
            pltpu.make_async_copy(
                g.at[pl.ds(pl.multiple_of(far_at + 96 * k, 96), 96), :],
                stack.at[pl.ds(256, 96), pl.ds(256 * k, 256)],
                sems.at[11 + k],
            )
        )
    for copy in lists + cut + bulk:
        copy.start()
    for copy in lists:
        copy.wait()
    row = row_held[...].reshape(1, OWN)
    kind = lax.broadcasted_iota(jnp.int32, (PACK - OWN, 128), 0)

    def spread(line):
        line = jnp.pad(line.astype(F32), ((0, 0), (0, PACK - OWN)))
        return jnp.concatenate([line, line], axis=1)

    high, low, scale = spread(row >> 5), spread(row & 31), spread(scale_held[...].reshape(1, OWN))
    text = jnp.where(kind == 0, high, jnp.where(kind == 1, low, jnp.where(kind == 2, scale, 0.0)))
    text = text.astype(BF16)
    for i in range(16):
        packs[i, OWN:, :] = text
    for i in range(8):
        cut[i].wait()
        packs[8 + i, :OWN, :] = packs[i, :OWN, :]
    for copy in bulk:
        copy.wait()


def keep(_, g, v, mine, v_kept):
    mine[...] = g[pl.ds(pl.multiple_of(lax.axis_index("core") * HALF, HALF), HALF), :]
    v_kept[...] = v[...]


def front(g, v, far, out):
    own = g[...]
    other = jnp.concatenate([far[256:, 256 * k : 256 * k + 256] for k in range(4)], axis=0)
    for j in range(4):
        cols = slice(256 * j, 256 * j + 256)
        part = dot(own, v[:, cols], 1, 0) + dot(other, far[:256, cols], 1, 0)
        part = part.astype(BF16)
        out[2 * j] = part[:, :128]
        out[2 * j + 1] = part[:, 128:]


def slope(recv, near, far, *outs):
    act = recv[0].astype(F32)
    for i in range(1, 8):
        act = act + recv[i].astype(F32)
    hidden = jnp.zeros((HALF, 128), F32)
    scale = jnp.zeros((HALF, 128), F32)
    token = lax.broadcasted_iota(jnp.int32, (HALF, 128), 0) + lax.axis_index("core") * HALF
    lane = lax.broadcasted_iota(jnp.int32, (1, 128), 1)
    valid = (lane % PACK) < OWN
    mirror = 8 * (1 - lax.axis_index("half"))
    for i in range(8):
        one, two = near[mirror + i], far[mirror + i]
        text = jnp.where(lane < PACK, one[OWN:].astype(F32), two[OWN:].astype(F32))
        rows = (text[0:1] * 32.0 + text[1:2]).astype(jnp.int32)
        hit = (token == rows) & valid
        codes = jnp.concatenate([one, two], axis=0)
        hidden = hidden + dot(jnp.where(hit, 1.0, 0.0).astype(BF16), codes, 1, 0)
        scale = scale + jnp.where(hit, text[2:3], 0.0)
    hidden = hidden * jnp.sum(scale, axis=1, keepdims=True)
    density = jnp.exp(-0.5 * hidden * hidden) * 0.3989422804014327
    cumulative = 0.5 * (1.0 + lax.erf(hidden * 0.7071067811865476))
    grad = (act * (cumulative + hidden * density)).astype(BF16)
    activated = (hidden * cumulative).astype(BF16)
    for i in range(8):
        outs[0][i, :HALF, :] = grad
        outs[-1][i, -HALF:, :] = activated


def input_part(hg, near, far, out):
    core = lax.axis_index("core")
    rows = jnp.concatenate([hg[i] for i in range(8)], axis=1)
    near_at = pl.multiple_of(256 * core, 256)
    far_at = pl.multiple_of(256 * (1 - core), 256)
    out[:, pl.ds(near_at, 256)] = dot(rows, near[...], 1, 1).astype(BF16)
    out[:, pl.ds(far_at, 256)] = dot(rows, far[...], 1, 1).astype(BF16)


def add_x(recv, mine, far, out):
    core, x = lax.axis_index("core"), lax.axis_index("x")
    total = recv[0].astype(F32)
    for i in range(1, 4):
        total = total + recv[i].astype(F32)
    out[...] = total.astype(BF16)

    @pl.when(lax.axis_index("zh") == 0)
    def _():
        own = mine[pl.ds(pl.multiple_of(x * 96, 96), 96), :].astype(F32)
        other = far[256:, pl.ds(pl.multiple_of(x * 256, 256), 256)].astype(F32)
        left = jnp.where(core == 0, own, other)
        right = jnp.where(core == 0, other, own)
        out[...] = (total + jnp.concatenate([left, right], axis=1)).astype(BF16)


def add_z(_, __, a, b, c, d, out):
    total = a[...].astype(F32) + b[...].astype(F32) + c[...].astype(F32) + d[...].astype(F32)
    total = total.astype(BF16)
    for i in range(4):
        out[i] = total[:, :256]
        out[4 + i] = total[:, 256:]


def split(both, first, last):
    first[...] = both[:, :HALF, :]
    last[...] = both[:, HALF:, :]


def finish(blocks, out):
    for i in range(8):
        out[96 * i : 96 * i + 96, :] = blocks[i]


def follow(*_):
    pass


def weights(left, near, far, out, after):
    after[...] = jnp.zeros_like(after)
    core = lax.axis_index("core")
    mine = left[pl.ds(pl.multiple_of(core * HALF, HALF), HALF), :].T
    other = left[pl.ds(pl.multiple_of((1 - core) * HALF, HALF), HALF), :].T
    for j in range(4):
        near_cols = jnp.concatenate([near[2 * j], near[2 * j + 1]], axis=1)
        far_cols = jnp.concatenate([far[2 * j], far[2 * j + 1]], axis=1)
        part = dot(mine, near_cols, 1, 0) + dot(other, far_cols, 1, 0)
        out[:, 256 * j : 256 * j + 256] = part.astype(BF16)


def shards(layer_input, w_up, w_down, parked_codes, parked_scales, parked_rows, incoming):
    packs, near = call(
        prepare, [((16, PACK, 128), BF16), ((STACK, 1024), BF16)],
        (parked_codes, parked_rows, parked_scales, incoming, w_down), in_specs=[HBM] * 5, nbytes=3 << 20,
        vmem=60, scratch=(pltpu.VMEM((OWN,), jnp.int32), pltpu.VMEM((OWN,), BF16), DMA((15,))),
    )
    ready = packs
    packs = lax.all_to_all(packs, ("half",) + CHIPS, 0, 0, tiled=True)
    packs_far = swap(packs, "core")
    far = swap(near, "core")
    u_far = swap(w_up, "core")

    mine, v = call(
        keep, [((HALF, 256), BF16), ((256, 1024), BF16)], (ready, incoming, w_down), vmem=24,
        in_specs=[ANY] + [VMEM] * 2,
    )
    sent = call(front, ((8, HALF, 128), BF16), (mine, v, far), vmem=24)
    recv = lax.all_to_all(sent, CHIPS, 0, 0, tiled=True)
    share = ((8, HALF, 128), BF16)
    wide = ((256, 1024), BF16)
    second = lax.axis_index("half") == 1

    def to_x(recv, packs, packs_far, u, u_far):
        hg, act = call(slope, [share, share], (recv, packs, packs_far), flops=1 << 27, nbytes=2 << 20)
        hg = lax.all_to_all(hg, CHIPS, 0, 0, tiled=True)
        part = call(
            input_part, ((HALF, 512), BF16), (hg, u, u_far),
            flops=2 * HALF * 512 * 1024, nbytes=3 << 20,
        )
        return lax.all_to_all(part.reshape(4, 96, 512), "x", 0, 0, tiled=True), hg, act

    def gather_both(recv, packs, packs_far, *_):
        both = call(
            slope, [((8, 2 * HALF, 128), BF16)], (recv, packs, packs_far), flops=1 << 27, nbytes=2 << 20
        )[0]
        both = lax.all_to_all(both, CHIPS, 0, 0, tiled=True)
        hg, act = call(split, [share, share], (both,))
        return jnp.zeros((4, 96, 512), BF16), hg, act

    part, hg, act = lax.cond(second, to_x, gather_both, recv, packs, packs_far, w_up, u_far)
    summed = call(add_x, ((96, 512), BF16), (part, mine, far), nbytes=1 << 20)
    got = [
        lax.ppermute(summed, ("half", "zh"), [(4 + i, (i + k) % 4) for i in range(4)])
        for k in range(4)
    ]

    def gradient(left, near):
        return call(
            weights, [wide, ((8, 128), F32)], (left, near, swap(near, "core")),
            flops=2 * TOK * 256 * 1024, nbytes=3 << 20,
        )

    def gradients(hg, act, x, g):
        up, first = gradient(x, hg)
        act = call(follow, share, (first, act), in_specs=[ANY, ANY], out_specs=ANY, input_output_aliases={1: 0})
        down, last = gradient(g, act)
        return up, down, first, last

    def gather_first(hg, act, x, g):
        return gradients(hg, lax.all_to_all(act, CHIPS, 0, 0, tiled=True), x, g)

    grad_up, grad_down, *after = lax.cond(second, gather_first, gradients, hg, act, layer_input, incoming)

    def spread_x(after, got):
        whole = call(add_z, ((8, 96, 256), BF16), (*after, *got), in_specs=[ANY] * 2 + [VMEM] * 4)
        passed = lax.all_to_all(whole, ("core", "x"), 0, 0, tiled=True)
        return call(finish, ((TOK, 256), BF16), (passed,))

    passed = lax.cond(second, lambda *_: jnp.zeros((TOK, 256), BF16), spread_x, after, got)
    return grad_up, grad_down, passed


def solution(mesh):
    fine = Mesh(mesh.devices.reshape(SHAPE), NAMES)
    return jax.shard_map(
        shards,
        mesh=fine,
        in_specs=(
            P(None, SECTION),
            P(SECTION, TENSOR),
            P(SECTION, TENSOR),
            P(SECTION, TENSOR),
            P(SECTION),
            P(SECTION),
            P(None, SECTION),
        ),
        out_specs=(P(SECTION, TENSOR), P(SECTION, TENSOR), P(None, SECTION)),
        check_vma=False,
    )
```

```python
import jax
import jax.numpy as jnp
from jax import lax
from jax.experimental import pallas as pl
from jax.experimental.pallas import tpu as pltpu
from jax.sharding import Mesh, PartitionSpec as P

SHAPE = (2, 2, 4, 2, 4, 4)
NAMES = ("half", "zb", "y", "core", "zh", "x")
SECTION = ("half", "zb", "y", "core")
TENSOR = ("zh", "x")
CHIPS = ("zb", "y")
F32 = jnp.float32
BF16 = jnp.bfloat16
TOK = 768
HALF = 384
OWN = 48
PACK = 64
STACK = 352
VMEM = pl.BlockSpec(memory_space=pltpu.VMEM)
ANY = pl.BlockSpec(memory_space=pl.ANY)
HBM = pl.BlockSpec(memory_space=pltpu.HBM)
DMA = pltpu.SemaphoreType.DMA


def call(kernel, outs, ins, scratch=(), flops=0, nbytes=0, vmem=48, **kwargs):
    many = isinstance(outs, list)
    shapes = [jax.ShapeDtypeStruct(shape, dtype) for shape, dtype in (outs if many else [outs])]
    kwargs.setdefault("in_specs", [VMEM] * len(ins))
    kwargs.setdefault("out_specs", [VMEM] * len(shapes) if many else VMEM)
    return pl.pallas_call(
        kernel,
        out_shape=shapes if many else shapes[0],
        scratch_shapes=list(scratch),
        compiler_params=pltpu.CompilerParams(vmem_limit_bytes=vmem << 20),
        cost_estimate=pl.CostEstimate(flops=flops, bytes_accessed=nbytes, transcendentals=0),
        **kwargs,
    )(*ins)


def swap(value, axis):
    return lax.ppermute(value, axis, [(0, 1), (1, 0)])


def dot(a, b, ca, cb):
    return lax.dot_general(a, b, (((ca,), (cb,)), ((), ())), preferred_element_type=F32)


def prepare(codes, rows, scales, g, v, packs, stack, row_held, scale_held, sems):
    far_at = (1 - lax.axis_index("core")) * HALF
    lists = [
        pltpu.make_async_copy(rows, row_held, sems.at[0]),
        pltpu.make_async_copy(scales, scale_held, sems.at[1]),
    ]
    cut = [
        pltpu.make_async_copy(
            codes.at[:, pl.ds(128 * i, 128)], packs.at[i, pl.ds(0, OWN), :], sems.at[2 + i]
        )
        for i in range(8)
    ]
    bulk = [pltpu.make_async_copy(v, stack.at[pl.ds(0, 256), :], sems.at[10])]
    for k in range(4):
        bulk.append(
            pltpu.make_async_copy(
                g.at[pl.ds(pl.multiple_of(far_at + 96 * k, 96), 96), :],
                stack.at[pl.ds(256, 96), pl.ds(256 * k, 256)],
                sems.at[11 + k],
            )
        )
    for copy in lists + cut + bulk:
        copy.start()
    for copy in lists:
        copy.wait()
    row = row_held[...].reshape(1, OWN)
    kind = lax.broadcasted_iota(jnp.int32, (PACK - OWN, 128), 0)

    def spread(line):
        line = jnp.pad(line.astype(F32), ((0, 0), (0, PACK - OWN)))
        return jnp.concatenate([line, line], axis=1)

    high, low, scale = spread(row >> 5), spread(row & 31), spread(scale_held[...].reshape(1, OWN))
    text = jnp.where(kind == 0, high, jnp.where(kind == 1, low, jnp.where(kind == 2, scale, 0.0)))
    text = text.astype(BF16)
    for i in range(16):
        packs[i, OWN:, :] = text
    for i in range(8):
        cut[i].wait()
        packs[8 + i, :OWN, :] = packs[i, :OWN, :]
    for copy in bulk:
        copy.wait()


def keep(_, g, v, mine, v_kept):
    mine[...] = g[pl.ds(pl.multiple_of(lax.axis_index("core") * HALF, HALF), HALF), :]
    v_kept[...] = v[...]


def front(g, v, far, out):
    own = g[...]
    other = jnp.concatenate([far[256:, 256 * k : 256 * k + 256] for k in range(4)], axis=0)
    for j in range(4):
        cols = slice(256 * j, 256 * j + 256)
        part = dot(own, v[:, cols], 1, 0) + dot(other, far[:256, cols], 1, 0)
        part = part.astype(BF16)
        out[2 * j] = part[:, :128]
        out[2 * j + 1] = part[:, 128:]


def slope(recv, near, far, *outs):
    act = recv[0].astype(F32)
    for i in range(1, 8):
        act = act + recv[i].astype(F32)
    hidden = jnp.zeros((HALF, 128), F32)
    scale = jnp.zeros((HALF, 128), F32)
    token = lax.broadcasted_iota(jnp.int32, (HALF, 128), 0) + lax.axis_index("core") * HALF
    lane = lax.broadcasted_iota(jnp.int32, (1, 128), 1)
    valid = (lane % PACK) < OWN
    mirror = 8 * (1 - lax.axis_index("half"))
    for i in range(8):
        one, two = near[mirror + i], far[mirror + i]
        text = jnp.where(lane < PACK, one[OWN:].astype(F32), two[OWN:].astype(F32))
        rows = (text[0:1] * 32.0 + text[1:2]).astype(jnp.int32)
        hit = (token == rows) & valid
        codes = jnp.concatenate([one, two], axis=0)
        hidden = hidden + dot(jnp.where(hit, 1.0, 0.0).astype(BF16), codes, 1, 0)
        scale = scale + jnp.where(hit, text[2:3], 0.0)
    hidden = hidden * jnp.sum(scale, axis=1, keepdims=True)
    density = jnp.exp(-0.5 * hidden * hidden) * 0.3989422804014327
    cumulative = 0.5 * (1.0 + lax.erf(hidden * 0.7071067811865476))
    grad = (act * (cumulative + hidden * density)).astype(BF16)
    activated = (hidden * cumulative).astype(BF16)
    if len(outs) == 1:
        for i in range(8):
            outs[0][i, :HALF, :] = grad
            outs[0][i, HALF:, :] = activated
        return
    grads, blocks, held, sem = outs
    held[...] = activated
    copy = pltpu.make_async_copy(held, blocks.at[0], sem)
    copy.start()
    for i in range(8):
        grads[i] = grad
    copy.wait()


def spread(blocks, out, held, sem):
    copy = pltpu.make_async_copy(blocks.at[0], held, sem)
    copy.start()
    copy.wait()
    for i in range(8):
        out[i] = held[...]


def input_part(hg, near, far, out):
    core = lax.axis_index("core")
    rows = jnp.concatenate([hg[i] for i in range(8)], axis=1)
    near_at = pl.multiple_of(256 * core, 256)
    far_at = pl.multiple_of(256 * (1 - core), 256)
    out[:, pl.ds(near_at, 256)] = dot(rows, near[...], 1, 1).astype(BF16)
    out[:, pl.ds(far_at, 256)] = dot(rows, far[...], 1, 1).astype(BF16)


def add_x(recv, mine, far, out):
    core, x = lax.axis_index("core"), lax.axis_index("x")
    total = recv[0].astype(F32)
    for i in range(1, 4):
        total = total + recv[i].astype(F32)
    out[...] = total.astype(BF16)

    @pl.when(lax.axis_index("zh") == 0)
    def _():
        own = mine[pl.ds(pl.multiple_of(x * 96, 96), 96), :].astype(F32)
        other = far[256:, pl.ds(pl.multiple_of(x * 256, 256), 256)].astype(F32)
        left = jnp.where(core == 0, own, other)
        right = jnp.where(core == 0, other, own)
        out[...] = (total + jnp.concatenate([left, right], axis=1)).astype(BF16)


def add_z(_, __, a, b, c, d, out):
    total = a[...].astype(F32) + b[...].astype(F32) + c[...].astype(F32) + d[...].astype(F32)
    total = total.astype(BF16)
    for i in range(4):
        out[i] = total[:, :256]
        out[4 + i] = total[:, 256:]


def split(both, first, last):
    first[...] = both[:, :HALF, :]
    last[...] = both[:, HALF:, :]


def finish(blocks, out):
    for i in range(8):
        out[96 * i : 96 * i + 96, :] = blocks[i]


def follow(*_):
    pass


def weights(left, near, far, out, after):
    after[...] = jnp.zeros_like(after)
    core = lax.axis_index("core")
    mine = left[pl.ds(pl.multiple_of(core * HALF, HALF), HALF), :].T
    other = left[pl.ds(pl.multiple_of((1 - core) * HALF, HALF), HALF), :].T
    for j in range(4):
        near_cols = jnp.concatenate([near[2 * j], near[2 * j + 1]], axis=1)
        far_cols = jnp.concatenate([far[2 * j], far[2 * j + 1]], axis=1)
        part = dot(mine, near_cols, 1, 0) + dot(other, far_cols, 1, 0)
        out[:, 256 * j : 256 * j + 256] = part.astype(BF16)


def shards(layer_input, w_up, w_down, parked_codes, parked_scales, parked_rows, incoming):
    packs, near = call(
        prepare, [((16, PACK, 128), BF16), ((STACK, 1024), BF16)],
        (parked_codes, parked_rows, parked_scales, incoming, w_down), in_specs=[HBM] * 5, nbytes=3 << 20,
        vmem=60, scratch=(pltpu.VMEM((OWN,), jnp.int32), pltpu.VMEM((OWN,), BF16), DMA((15,))),
    )
    ready = packs
    packs = lax.all_to_all(packs, ("half",) + CHIPS, 0, 0, tiled=True)
    packs_far = swap(packs, "core")
    far = swap(near, "core")
    u_far = swap(w_up, "core")

    mine, v = call(
        keep, [((HALF, 256), BF16), ((256, 1024), BF16)], (ready, incoming, w_down), vmem=24,
        in_specs=[ANY] + [VMEM] * 2,
    )
    sent = call(front, ((8, HALF, 128), BF16), (mine, v, far), vmem=24)
    recv = lax.all_to_all(sent, CHIPS, 0, 0, tiled=True)
    share = ((8, HALF, 128), BF16)
    wide = ((256, 1024), BF16)
    second = lax.axis_index("half") == 1

    def to_x(recv, packs, packs_far, u, u_far):
        hg, act = call(
            slope, [share, share], (recv, packs, packs_far), flops=1 << 27, nbytes=2 << 20,
            out_specs=[VMEM, HBM], scratch=(pltpu.VMEM((HALF, 128), BF16), DMA),
        )
        hg = lax.all_to_all(hg, CHIPS, 0, 0, tiled=True)
        part = call(
            input_part, ((HALF, 512), BF16), (hg, u, u_far),
            flops=2 * HALF * 512 * 1024, nbytes=3 << 20,
        )
        return lax.all_to_all(part.reshape(4, 96, 512), "x", 0, 0, tiled=True), hg, act

    def gather_both(recv, packs, packs_far, *_):
        both = call(
            slope, [((8, 2 * HALF, 128), BF16)], (recv, packs, packs_far), flops=1 << 27, nbytes=2 << 20
        )[0]
        both = lax.all_to_all(both, CHIPS, 0, 0, tiled=True)
        hg, act = call(split, [share, share], (both,))
        return jnp.zeros((4, 96, 512), BF16), hg, act

    part, hg, act = lax.cond(second, to_x, gather_both, recv, packs, packs_far, w_up, u_far)
    summed = call(add_x, ((96, 512), BF16), (part, mine, far), nbytes=1 << 20)
    got = [
        lax.ppermute(summed, ("half", "zh"), [(4 + i, (i + k) % 4) for i in range(4)])
        for k in range(4)
    ]

    def gradient(left, near):
        return call(
            weights, [wide, ((8, 128), F32)], (left, near, swap(near, "core")),
            flops=2 * TOK * 256 * 1024, nbytes=3 << 20,
        )

    def gradients(hg, act, x, g):
        up, first = gradient(x, hg)
        act = call(follow, share, (first, act), in_specs=[ANY, ANY], out_specs=ANY, input_output_aliases={1: 0})
        down, last = gradient(g, act)
        return up, down, first, last

    def gather_first(hg, act, x, g):
        act = call(spread, share, (act,), in_specs=[HBM], scratch=(pltpu.VMEM((HALF, 128), BF16), DMA))
        return gradients(hg, lax.all_to_all(act, CHIPS, 0, 0, tiled=True), x, g)

    grad_up, grad_down, *after = lax.cond(second, gather_first, gradients, hg, act, layer_input, incoming)

    def spread_x(after, got):
        whole = call(add_z, ((8, 96, 256), BF16), (*after, *got), in_specs=[ANY] * 2 + [VMEM] * 4)
        passed = lax.all_to_all(whole, ("core", "x"), 0, 0, tiled=True)
        return call(finish, ((TOK, 256), BF16), (passed,))

    passed = lax.cond(second, lambda *_: jnp.zeros((TOK, 256), BF16), spread_x, after, got)
    return grad_up, grad_down, passed


def solution(mesh):
    fine = Mesh(mesh.devices.reshape(SHAPE), NAMES)
    return jax.shard_map(
        shards,
        mesh=fine,
        in_specs=(
            P(None, SECTION),
            P(SECTION, TENSOR),
            P(SECTION, TENSOR),
            P(SECTION, TENSOR),
            P(SECTION),
            P(SECTION),
            P(None, SECTION),
        ),
        out_specs=(P(SECTION, TENSOR), P(SECTION, TENSOR), P(None, SECTION)),
        check_vma=False,
    )
```

```python
import jax
import jax.numpy as jnp
from jax import lax
from jax.experimental import pallas as pl
from jax.experimental.pallas import tpu as pltpu
from jax.sharding import Mesh, PartitionSpec as P

SHAPE = (2, 2, 4, 2, 4, 4)
NAMES = ("half", "zb", "y", "core", "zh", "x")
SECTION = ("half", "zb", "y", "core")
TENSOR = ("zh", "x")
CHIPS = ("zb", "y")
F32 = jnp.float32
BF16 = jnp.bfloat16
TOK = 768
HALF = 384
OWN = 48
PACK = 64
STACK = 352
VMEM = pl.BlockSpec(memory_space=pltpu.VMEM)
ANY = pl.BlockSpec(memory_space=pl.ANY)
HBM = pl.BlockSpec(memory_space=pltpu.HBM)
DMA = pltpu.SemaphoreType.DMA


def call(kernel, outs, ins, scratch=(), flops=0, nbytes=0, vmem=20, **kwargs):
    many = isinstance(outs, list)
    shapes = [jax.ShapeDtypeStruct(shape, dtype) for shape, dtype in (outs if many else [outs])]
    kwargs.setdefault("in_specs", [VMEM] * len(ins))
    kwargs.setdefault("out_specs", [VMEM] * len(shapes) if many else VMEM)
    return pl.pallas_call(
        kernel,
        out_shape=shapes if many else shapes[0],
        scratch_shapes=list(scratch),
        compiler_params=pltpu.CompilerParams(vmem_limit_bytes=vmem << 20),
        cost_estimate=pl.CostEstimate(flops=flops, bytes_accessed=nbytes, transcendentals=0),
        **kwargs,
    )(*ins)


def swap(value, axis):
    return lax.ppermute(value, axis, [(0, 1), (1, 0)])


def dot(a, b, ca, cb):
    return lax.dot_general(a, b, (((ca,), (cb,)), ((), ())), preferred_element_type=F32)


def prepare(codes, rows, scales, g, v, packs, stack, row_held, scale_held, sems):
    far_at = (1 - lax.axis_index("core")) * HALF
    lists = [
        pltpu.make_async_copy(rows, row_held, sems.at[0]),
        pltpu.make_async_copy(scales, scale_held, sems.at[1]),
    ]
    cut = [
        pltpu.make_async_copy(
            codes.at[:, pl.ds(128 * i, 128)], packs.at[i, pl.ds(0, OWN), :], sems.at[2 + i]
        )
        for i in range(8)
    ]
    bulk = [pltpu.make_async_copy(v, stack.at[pl.ds(0, 256), :], sems.at[10])]
    for k in range(4):
        bulk.append(
            pltpu.make_async_copy(
                g.at[pl.ds(pl.multiple_of(far_at + 96 * k, 96), 96), :],
                stack.at[pl.ds(256, 96), pl.ds(256 * k, 256)],
                sems.at[11 + k],
            )
        )
    for copy in lists + cut + bulk:
        copy.start()
    for copy in lists:
        copy.wait()
    row = row_held[...].reshape(1, OWN)
    kind = lax.broadcasted_iota(jnp.int32, (PACK - OWN, 128), 0)

    def spread(line):
        line = jnp.pad(line.astype(F32), ((0, 0), (0, PACK - OWN)))
        return jnp.concatenate([line, line], axis=1)

    high, low, scale = spread(row >> 5), spread(row & 31), spread(scale_held[...].reshape(1, OWN))
    text = jnp.where(kind == 0, high, jnp.where(kind == 1, low, jnp.where(kind == 2, scale, 0.0)))
    text = text.astype(BF16)
    for i in range(16):
        packs[i, OWN:, :] = text
    for i in range(8):
        cut[i].wait()
        packs[8 + i, :OWN, :] = packs[i, :OWN, :]
    for copy in bulk:
        copy.wait()


def keep(_, g, v, mine, v_kept):
    mine[...] = g[pl.ds(pl.multiple_of(lax.axis_index("core") * HALF, HALF), HALF), :]
    v_kept[...] = v[...]


def front(g, v, far, out):
    own = g[...]
    other = jnp.concatenate([far[256:, 256 * k : 256 * k + 256] for k in range(4)], axis=0)
    for j in range(4):
        cols = slice(256 * j, 256 * j + 256)
        part = dot(own, v[:, cols], 1, 0) + dot(other, far[:256, cols], 1, 0)
        part = part.astype(BF16)
        out[2 * j] = part[:, :128]
        out[2 * j + 1] = part[:, 128:]


def slope(recv, near, far, *outs):
    act = recv[0].astype(F32)
    for i in range(1, 8):
        act = act + recv[i].astype(F32)
    hidden = jnp.zeros((HALF, 128), F32)
    scale = jnp.zeros((HALF, 128), F32)
    token = lax.broadcasted_iota(jnp.int32, (HALF, 128), 0) + lax.axis_index("core") * HALF
    lane = lax.broadcasted_iota(jnp.int32, (1, 128), 1)
    valid = (lane % PACK) < OWN
    mirror = 8 * (1 - lax.axis_index("half"))
    for i in range(8):
        one, two = near[mirror + i], far[mirror + i]
        text = jnp.where(lane < PACK, one[OWN:].astype(F32), two[OWN:].astype(F32))
        rows = (text[0:1] * 32.0 + text[1:2]).astype(jnp.int32)
        hit = (token == rows) & valid
        codes = jnp.concatenate([one, two], axis=0)
        hidden = hidden + dot(jnp.where(hit, 1.0, 0.0).astype(BF16), codes, 1, 0)
        scale = scale + jnp.where(hit, text[2:3], 0.0)
    hidden = hidden * jnp.sum(scale, axis=1, keepdims=True)
    density = jnp.exp(-0.5 * hidden * hidden) * 0.3989422804014327
    cumulative = 0.5 * (1.0 + lax.erf(hidden * 0.7071067811865476))
    grad = (act * (cumulative + hidden * density)).astype(BF16)
    activated = (hidden * cumulative).astype(BF16)
    if len(outs) == 1:
        for i in range(8):
            outs[0][i, :HALF, :] = grad
            outs[0][i, HALF:, :] = activated
        return
    grads, blocks, held, sem = outs
    held[...] = activated
    copy = pltpu.make_async_copy(held, blocks.at[0], sem)
    copy.start()
    for i in range(8):
        grads[i] = grad
    copy.wait()


def spread(blocks, out, held, sem):
    copy = pltpu.make_async_copy(blocks.at[0], held, sem)
    copy.start()
    copy.wait()
    for i in range(8):
        out[i] = held[...]


def input_part(hg, near, far, out):
    core = lax.axis_index("core")
    rows = jnp.concatenate([hg[i] for i in range(8)], axis=1)
    near_at = pl.multiple_of(256 * core, 256)
    far_at = pl.multiple_of(256 * (1 - core), 256)
    out[:, pl.ds(near_at, 256)] = dot(rows, near[...], 1, 1).astype(BF16)
    out[:, pl.ds(far_at, 256)] = dot(rows, far[...], 1, 1).astype(BF16)


def add_x(recv, mine, far, out):
    core, x = lax.axis_index("core"), lax.axis_index("x")
    total = recv[0].astype(F32)
    for i in range(1, 4):
        total = total + recv[i].astype(F32)
    out[...] = total.astype(BF16)

    @pl.when(lax.axis_index("zh") == 0)
    def _():
        own = mine[pl.ds(pl.multiple_of(x * 96, 96), 96), :].astype(F32)
        other = far[256:, pl.ds(pl.multiple_of(x * 256, 256), 256)].astype(F32)
        left = jnp.where(core == 0, own, other)
        right = jnp.where(core == 0, other, own)
        out[...] = (total + jnp.concatenate([left, right], axis=1)).astype(BF16)


def add_z(_, __, a, b, c, d, out):
    total = a[...].astype(F32) + b[...].astype(F32) + c[...].astype(F32) + d[...].astype(F32)
    total = total.astype(BF16)
    for i in range(4):
        out[i] = total[:, :256]
        out[4 + i] = total[:, 256:]


def split(both, first, last):
    first[...] = both[:, :HALF, :]
    last[...] = both[:, HALF:, :]


def finish(blocks, out):
    for i in range(8):
        out[96 * i : 96 * i + 96, :] = blocks[i]


def follow(*_):
    pass


def weights(left, near, far, out, after):
    after[...] = jnp.zeros_like(after)
    core = lax.axis_index("core")
    mine = left[pl.ds(pl.multiple_of(core * HALF, HALF), HALF), :].T
    other = left[pl.ds(pl.multiple_of((1 - core) * HALF, HALF), HALF), :].T
    for j in range(4):
        near_cols = jnp.concatenate([near[2 * j], near[2 * j + 1]], axis=1)
        far_cols = jnp.concatenate([far[2 * j], far[2 * j + 1]], axis=1)
        part = dot(mine, near_cols, 1, 0) + dot(other, far_cols, 1, 0)
        out[:, 256 * j : 256 * j + 256] = part.astype(BF16)


def shards(layer_input, w_up, w_down, parked_codes, parked_scales, parked_rows, incoming):
    packs, near = call(
        prepare, [((16, PACK, 128), BF16), ((STACK, 1024), BF16)],
        (parked_codes, parked_rows, parked_scales, incoming, w_down), in_specs=[HBM] * 5, nbytes=3 << 20,
        vmem=60, scratch=(pltpu.VMEM((OWN,), jnp.int32), pltpu.VMEM((OWN,), BF16), DMA((15,))),
    )
    ready = packs
    packs = lax.all_to_all(packs, ("half",) + CHIPS, 0, 0, tiled=True)
    packs_far = swap(packs, "core")
    far = swap(near, "core")
    u_far = swap(w_up, "core")

    mine, v = call(
        keep, [((HALF, 256), BF16), ((256, 1024), BF16)], (ready, incoming, w_down), vmem=24,
        in_specs=[ANY] + [VMEM] * 2,
    )
    sent = call(front, ((8, HALF, 128), BF16), (mine, v, far), vmem=24)
    recv = lax.all_to_all(sent, CHIPS, 0, 0, tiled=True)
    share = ((8, HALF, 128), BF16)
    wide = ((256, 1024), BF16)
    second = lax.axis_index("half") == 1

    def to_x(recv, packs, packs_far, u, u_far):
        hg, act = call(
            slope, [share, share], (recv, packs, packs_far), flops=1 << 27, nbytes=2 << 20,
            out_specs=[VMEM, HBM], scratch=(pltpu.VMEM((HALF, 128), BF16), DMA),
        )
        hg = lax.all_to_all(hg, CHIPS, 0, 0, tiled=True)
        part = call(
            input_part, ((HALF, 512), BF16), (hg, u, u_far),
            flops=2 * HALF * 512 * 1024, nbytes=3 << 20,
        )
        return lax.all_to_all(part.reshape(4, 96, 512), "x", 0, 0, tiled=True), hg, act

    def gather_both(recv, packs, packs_far, *_):
        both = call(
            slope, [((8, 2 * HALF, 128), BF16)], (recv, packs, packs_far), flops=1 << 27, nbytes=2 << 20
        )[0]
        both = lax.all_to_all(both, CHIPS, 0, 0, tiled=True)
        hg, act = call(split, [share, share], (both,))
        return jnp.zeros((4, 96, 512), BF16), hg, act

    part, hg, act = lax.cond(second, to_x, gather_both, recv, packs, packs_far, w_up, u_far)
    summed = call(add_x, ((96, 512), BF16), (part, mine, far), nbytes=1 << 20)
    got = [
        lax.ppermute(summed, ("half", "zh"), [(4 + i, (i + k) % 4) for i in range(4)])
        for k in range(4)
    ]

    def gradient(left, near):
        return call(
            weights, [wide, ((8, 128), F32)], (left, near, swap(near, "core")),
            flops=2 * TOK * 256 * 1024, nbytes=3 << 20,
        )

    def gradients(hg, act, x, g):
        up, first = gradient(x, hg)
        act = call(follow, share, (first, act), in_specs=[ANY, ANY], out_specs=ANY, input_output_aliases={1: 0})
        down, last = gradient(g, act)
        return up, down, first, last

    def gather_first(hg, act, x, g):
        act = call(spread, share, (act,), in_specs=[HBM], scratch=(pltpu.VMEM((HALF, 128), BF16), DMA))
        return gradients(hg, lax.all_to_all(act, CHIPS, 0, 0, tiled=True), x, g)

    grad_up, grad_down, *after = lax.cond(second, gather_first, gradients, hg, act, layer_input, incoming)

    def spread_x(after, got):
        whole = call(add_z, ((8, 96, 256), BF16), (*after, *got), in_specs=[ANY] * 2 + [VMEM] * 4)
        passed = lax.all_to_all(whole, ("core", "x"), 0, 0, tiled=True)
        return call(finish, ((TOK, 256), BF16), (passed,))

    passed = lax.cond(second, lambda *_: jnp.zeros((TOK, 256), BF16), spread_x, after, got)
    return grad_up, grad_down, passed


def solution(mesh):
    fine = Mesh(mesh.devices.reshape(SHAPE), NAMES)
    return jax.shard_map(
        shards,
        mesh=fine,
        in_specs=(
            P(None, SECTION),
            P(SECTION, TENSOR),
            P(SECTION, TENSOR),
            P(SECTION, TENSOR),
            P(SECTION),
            P(SECTION),
            P(None, SECTION),
        ),
        out_specs=(P(SECTION, TENSOR), P(SECTION, TENSOR), P(None, SECTION)),
        check_vma=False,
    )
```
